128 devices in a mesh: dp: 4 (over z), pipe: 8 (over y, x_lo), tensor: 4 (over x_hi, core).
Axes of the slice: x: 4 (x_hi: 2, x_lo: 2; x = x_hi * 2 + x_lo), y: 4, z: 4, core: 2. Of those that a mesh axis runs over, the one named last changes fastest.
Arguments:
- vision: bfloat16 [1024, 8192], P('dp', 'tensor'), may hold values from -6 to 6
- features: bfloat16 [1024, 7680], P('dp'), may hold values from -6 to 6
- queries: bfloat16 [2048, 8192], P('dp', 'tensor'), may hold values from -4 to 4
- ctx_grad: bfloat16 [2048, 8192], P('dp', 'tensor'), may hold values from -4 to 4
- row_mask: int32 [2048], P('dp'), may hold values 0 or 1
- key_weight: bfloat16 [8, 8192, 1024], P('pipe', None, 'tensor'), may hold values from -0.0625 to 0.0625
- value_weight: bfloat16 [8, 8192, 1024], P('pipe', None, 'tensor'), may hold values from -0.0625 to 0.0625
- key_gain: float32 [8, 128], P('pipe'), may hold values from 0.1 to 1.9
Outputs:
- key_weight_grad: float32 [8, 8192, 1024], P('pipe', 'dp', 'tensor')
- value_weight_grad: float32 [8, 8192, 1024], P('pipe', 'dp', 'tensor')
- projector_grad: float32 [7680, 8192], P('dp', ('pipe', 'tensor'))
The draws below stay inside these ranges and needn't reach their ends.
All inputs are finite; a program needn't handle non-finite values. No bound on the sum of `row_mask` on one device may be relied on, other than what follows from the above.
Results may differ from the reference program's by a relative error of at most 0.009.
Values may be sent and summed in bfloat16 or wider, within the bound.
No kernel may reach another device: no remote copies, remote signals or barrier semaphores. Data moves between devices by JAX's collectives and lax.ppermute only.
A program may use at most 128 MiB of HBM per device.

```python
import jax
import jax.numpy as jnp
from jax import lax

D = 8192
DV = 7680
H = 64
KVH = 8
HD = 128
TXT = 512
VIS = 256
LAYERS = 8
TXT_ALL = 2048
VIS_ALL = 1024
N_DP = 4


def with_ends(result, rng, smallest, top_value):
    shape = result.shape
    place = [jax.random.randint(jax.random.fold_in(rng, axis), (), 0, shape[axis]) for axis in range(len(shape))]
    result = result.at[tuple(place)].set(smallest)
    longest = shape.index(max(shape))
    place[longest] = (place[longest] + 1) % shape[longest]
    return result.at[tuple(place)].set(top_value)


def steps_of(stream_key, shape, cuts, least, top_value):
    factor_of = 1.0
    for position, blocks in cuts:
        steps = jax.random.uniform(jax.random.fold_in(jax.random.fold_in(stream_key, 6), position), (blocks,), jnp.float32, least / len(cuts), top_value / len(cuts))
        factor_of = factor_of * jnp.repeat(jnp.exp(steps), shape[position] // blocks).reshape((-1,) + (1,) * (len(shape) - 1 - position))
    return factor_of


def gaussian(stream_key, dims, spread, most, cuts=(), held_as=jnp.bfloat16):
    loudness = steps_of(stream_key, dims, cuts, -0.22, 0.18) if cuts else 1.0
    values = jax.random.normal(stream_key, dims, jnp.float32) * spread * loudness
    return jnp.minimum(jnp.maximum(values, -most), most).astype(held_as)


def setup_inputs(seed: int = 0) -> dict:
    arg_keys = jax.random.split(jax.random.key(seed), 9)
    return {
        "vision": gaussian(arg_keys[0], (VIS_ALL, D), 1.0, 6.0, ((0, 4), (1, 4))),
        "features": gaussian(arg_keys[1], (VIS_ALL, DV), 1.0, 6.0, ((0, 4),)),
        "queries": gaussian(arg_keys[2], (TXT_ALL, H * HD), 1.0, 4.0, ((0, 4), (1, 4))),
        "ctx_grad": gaussian(arg_keys[3], (TXT_ALL, H * HD), 0.25, 4.0, ((0, 4), (1, 4))),
        "row_mask": with_ends((jax.random.randint(arg_keys[4], (TXT_ALL,), 0, 4) < 3).astype(jnp.int32), jax.random.fold_in(arg_keys[4], 1), 0, 1),
        "key_weight": gaussian(arg_keys[5], (LAYERS, D, KVH * HD), D ** -0.5, 0.0625, ((0, 8), (2, 4))),
        "value_weight": gaussian(arg_keys[6], (LAYERS, D, KVH * HD), D ** -0.5, 0.0625, ((0, 8), (2, 4))),
        "key_gain": jnp.clip(1.0 + 0.18 * jax.random.normal(arg_keys[7], (LAYERS, HD), jnp.float32), 0.1, 1.9),
    }


norm_eps = 1e-05

def local_grads(vision_rows, queries, ctx_grad, row_mask, key_proj, value_proj, key_gain):
    head_size = key_gain.shape[0]
    vis_rows = vision_rows.shape[0]
    text_rows = queries.shape[0]
    kv_heads = key_proj.shape[1] // head_size
    group_size = queries.shape[1] // head_size // kv_heads
    score_scale = head_size ** (-0.5)
    key_raw = jnp.dot(vision_rows, key_proj, preferred_element_type=jnp.float32).reshape(vis_rows, kv_heads, head_size)
    inv_rms = lax.rsqrt(lax.optimization_barrier(jnp.mean(key_raw * key_raw, -1, keepdims=True)) + norm_eps)
    keys = (key_raw * inv_rms * key_gain).astype(jnp.bfloat16).astype(jnp.float32)
    values = jnp.dot(vision_rows, value_proj, preferred_element_type=jnp.float32).astype(jnp.bfloat16)
    values = values.astype(jnp.float32).reshape(vis_rows, kv_heads, head_size)
    query_heads = queries.astype(jnp.float32).reshape(text_rows, kv_heads, group_size, head_size)
    masked = (ctx_grad * row_mask[:, None].astype(jnp.bfloat16)).astype(jnp.float32)
    masked = masked.reshape(text_rows, kv_heads, group_size, head_size)
    scores = jnp.einsum('tkgd,vkd->kgtv', query_heads, keys) * score_scale
    exp_scores = jnp.exp(scores)
    attn_probs = exp_scores / lax.optimization_barrier(jnp.sum(exp_scores, -1, keepdims=True))
    probs_bf = attn_probs.astype(jnp.bfloat16).astype(jnp.float32)
    context = jnp.einsum('kgtv,vkd->tkgd', probs_bf, values)
    row_delta = lax.optimization_barrier(jnp.sum(masked * context, -1)).transpose(1, 2, 0)[..., None]
    value_grad = jnp.einsum('kgtv,tkgd->vkd', probs_bf, masked).astype(jnp.bfloat16)
    prob_grad = jnp.einsum('tkgd,vkd->kgtv', masked, values)
    score_grad = (attn_probs * (prob_grad - row_delta) * score_scale).astype(jnp.bfloat16).astype(jnp.float32)
    normed_grad = jnp.einsum('kgtv,tkgd->vkd', score_grad, query_heads)
    scaled = normed_grad * key_gain
    key_grad = inv_rms * (scaled - key_raw * inv_rms * inv_rms * lax.optimization_barrier(jnp.mean(scaled * key_raw, -1, keepdims=True)))
    key_grad = key_grad.astype(jnp.bfloat16)
    return (key_grad.reshape(vis_rows, -1), value_grad.reshape(vis_rows, -1))

def reference(vision, features, queries, ctx_grad, row_mask, key_weight, value_weight, key_gain):
    key_total = jnp.zeros(key_weight.shape, jnp.float32)
    value_total = jnp.zeros(value_weight.shape, jnp.float32)
    projector_total = jnp.zeros((features.shape[1], vision.shape[1]), jnp.float32)
    for replica in range(N_DP):
        vision_rows = vision[replica * VIS:(replica + 1) * VIS]
        feature_rows = features[replica * VIS:(replica + 1) * VIS]
        query_rows = queries[replica * TXT:(replica + 1) * TXT]
        grad_rows = ctx_grad[replica * TXT:(replica + 1) * TXT]
        mask_rows = row_mask[replica * TXT:(replica + 1) * TXT]
        summed = jnp.zeros(vision_rows.shape, jnp.float32)
        for layer_index in range(LAYERS):
            key_grad, value_grad = local_grads(vision_rows, query_rows, grad_rows, mask_rows, key_weight[layer_index], value_weight[layer_index], key_gain[layer_index])
            key_term = jnp.dot(vision_rows.T, key_grad, preferred_element_type=jnp.float32)
            value_term = jnp.dot(vision_rows.T, value_grad, preferred_element_type=jnp.float32)
            key_total = key_total.at[layer_index].add(key_term)
            value_total = value_total.at[layer_index].add(value_term)
            summed = summed + jnp.dot(key_grad, key_weight[layer_index].T, preferred_element_type=jnp.float32)
            summed = summed + jnp.dot(value_grad, value_weight[layer_index].T, preferred_element_type=jnp.float32)
        projector_total = projector_total + jnp.dot(feature_rows.T, summed.astype(jnp.bfloat16), preferred_element_type=jnp.float32)
    return (key_total, value_total, projector_total)
```

```python
import jax
import jax.numpy as jnp
from jax import lax
from jax.experimental import pallas as pl
from jax.experimental.pallas import tpu as pltpu
from jax.sharding import PartitionSpec as P

norm_eps = 1e-05
every_axis = ("dp", "pipe", "tensor")
bf16 = jnp.bfloat16
f32 = jnp.float32
head_size = 128
score_scale = head_size**-0.5
log2_e = 1.4426950408889634
megabyte = 2**20


def flat_index(z, y, x, core):
    return z * 32 + y * 8 + (x & 1) * 4 + (x >> 1) * 2 + core


def exchange_pairs(moved):
    pairs = []
    for z in range(4):
        for y in range(4):
            for x in range(4):
                for core in range(2):
                    pairs.append((flat_index(z, y, x, core), flat_index(*moved(z, y, x, core))))
    return pairs


def send(array, moved):
    return lax.ppermute(array, every_axis, exchange_pairs(moved))


def to_core(z, y, x, core):
    return z, y, x, 1 - core


def to_near_x(z, y, x, core):
    return z, y, x ^ 3, core


def first_stage(k):
    return lambda z, y, x, core: (z, y, x ^ k, core) if core == 0 else (z, y ^ k, x, core)


def second_stage(k):
    return lambda z, y, x, core: (z, y ^ k, x, core) if core == 0 else (z, y, x ^ k, core)


def along_z(k):
    return lambda z, y, x, core: (z ^ k, y, x, core)


def near_z(z, y, x, core):
    return (z ^ 1 if core == 0 else z ^ 3), y, x, core


params = pltpu.CompilerParams(vmem_limit_bytes=20 * megabyte)
large_params = pltpu.CompilerParams(vmem_limit_bytes=40 * megabyte)
def dot(left, right, left_dim=1, right_dim=0):
    return lax.dot_general(
        left, right, (((left_dim,), (right_dim,)), ((), ())), preferred_element_type=f32
    )


in_vmem = pl.BlockSpec(memory_space=pltpu.VMEM)
in_smem = pl.BlockSpec(memory_space=pltpu.SMEM)


in_hbm = pl.BlockSpec(memory_space=pltpu.HBM)


def far_away(array):
    return pltpu.with_memory_space_constraint(array, pltpu.HBM)


def chosen_spec(rows, columns, k, place):
    return pl.BlockSpec(
        (rows, columns), lambda i, table: (0, jnp.where(table[place] == k, i, 0))
    )


def cut_features(features, table):
    rows, width = features.shape
    width //= 4
    half = rows // 2

    def kernel(table, near_in, far_in, near_out, far_out):
        near_out[...] = near_in[...]
        far_out[...] = far_in[...]

    return pl.pallas_call(
        kernel,
        grid_spec=pltpu.PrefetchScalarGridSpec(
            num_scalar_prefetch=1,
            grid=(2,),
            in_specs=[
                pl.BlockSpec((half, width), lambda i, table: (i, table[0])),
                pl.BlockSpec((half // 2, width), lambda i, table: (2 * table[2] + i, table[1])),
            ],
            out_specs=[
                pl.BlockSpec((half, width), lambda i, table: (i, 0)),
                pl.BlockSpec((half // 2, width), lambda i, table: (i, 0)),
            ],
        ),
        out_shape=[jax.ShapeDtypeStruct((r, width), bf16) for r in (rows, half)],
        compiler_params=params,
        name="cut_features",
    )(table, far_away(features), far_away(features))


def project(slices, positions, key_proj, value_proj, start=None):
    rows, width = slices[0].shape
    columns = key_proj.shape[1]
    n = len(slices)

    def kernel(table, *refs):
        slice_refs, projections, rest = refs[:n], refs[n : n + 2], refs[n + 2 :]
        out, held, sems = rest[-3:]
        copies = []
        for i in range(n):
            lines = pl.ds(pl.multiple_of(table[i] * width, width), width)
            for j in range(2):
                copy = pltpu.make_async_copy(projections[j].at[lines, :], held.at[i, j], sems.at[i, j])
                copy.start()
                copies.append(copy)
        for j in range(2):
            place = slice(j * columns, (j + 1) * columns)
            total = 0.0 if start is None else rest[0][:, place]
            for i in range(n):
                copies[2 * i + j].wait()
                total += dot(slice_refs[i][...], held[i, j])
            out[:, place] = total

    operands = [*slices, far_away(key_proj), far_away(value_proj)]
    if start is not None:
        operands.append(start)
    return pl.pallas_call(
        kernel,
        in_specs=[in_smem] + [in_vmem] * n + [in_hbm] * 2 + [in_vmem] * (len(operands) - n - 2),
        out_specs=in_vmem,
        out_shape=jax.ShapeDtypeStruct((rows, 2 * columns), f32),
        scratch_shapes=[pltpu.VMEM((n, 2, width, columns), bf16), pltpu.SemaphoreType.DMA((n, 2))],
        compiler_params=params,
        name="project",
    )(positions, *operands)


def choose(slices, table):
    rows, width = slices[0].shape
    half = rows // 2

    def kernel(table, *refs):
        near, far = refs[4:]
        for k in range(4):

            @pl.when(table[0] == k)
            def _():
                near[...] = refs[k][...]

            @pl.when(table[1] == k)
            def _():
                far[...] = refs[k][pl.ds(pl.multiple_of(table[2] * half, half), half), :]

    return pl.pallas_call(
        kernel,
        in_specs=[in_smem] + [in_vmem] * 4,
        out_specs=[in_vmem] * 2,
        out_shape=[jax.ShapeDtypeStruct((r, width), bf16) for r in (rows, half)],
        compiler_params=params,
        name="choose",
    )(table, *slices)


def middle(last_slice, raw, queries, masked, gain, key_proj, value_proj, table):
    vis_rows, width = last_slice.shape
    depth, columns = key_proj.shape
    kv_heads = columns // head_size
    text_rows = queries.shape[0]
    group = queries.shape[1] // head_size // kv_heads
    group_width = group * head_size
    half = vis_rows // 2
    slices = depth // width
    blocks = 16
    lines = depth // blocks
    unroll = 4

    def kernel(
        table, slice_ref, raw_ref, gain_ref, query_hbm, masked_hbm, key_hbm, value_hbm,
        grads, other_terms, own_terms,
        weights, query_ref, masked_ref, keys, values, sums, turned, text_sems, weight_sems,
    ):
        def weight_copies(i):
            place = pl.ds(pl.multiple_of(table[i] * width, width), width)
            return [
                pltpu.make_async_copy(source.at[place, :], weights.at[j, place, :], weight_sems.at[i, j])
                for j, source in enumerate((key_hbm, value_hbm))
            ]

        def text_copies(head):
            place = pl.ds(head * group_width, group_width)
            return [
                pltpu.make_async_copy(source.at[:, place], target.at[head], text_sems.at[head, j])
                for j, (source, target) in enumerate(((query_hbm, query_ref), (masked_hbm, masked_ref)))
            ]

        all_weight_copies = [weight_copies(i) for i in range(slices)]
        all_text_copies = [text_copies(head) for head in range(kv_heads)]
        for copy in all_weight_copies[0] + sum(all_text_copies, []) + sum(all_weight_copies[1:], []):
            copy.start()
        for copy in all_weight_copies[0]:
            copy.wait()
        place = pl.ds(pl.multiple_of(table[0] * width, width), width)
        key_all = raw_ref[:, :columns] + dot(slice_ref[...], weights[0, place, :])
        value_all = (raw_ref[:, columns:] + dot(slice_ref[...], weights[1, place, :])).astype(bf16)
        for head in range(kv_heads):
            lanes = slice(head * head_size, (head + 1) * head_size)
            key_raw = key_all[:, lanes]
            inv_rms = lax.rsqrt(jnp.mean(key_raw * key_raw, -1, keepdims=True) + norm_eps)
            keys[...] = (key_raw * inv_rms * gain_ref[...]).astype(bf16)
            values[...] = value_all[:, lanes]
            sums[...] = jnp.zeros_like(sums)
            for copy in all_text_copies[head]:
                copy.wait()

            def step(i, carry):
                for j in range(unroll):
                    text = pl.ds(pl.multiple_of((i * unroll + j) * head_size, head_size), head_size)
                    query = query_ref[head, :, text]
                    grad = masked_ref[head, :, text]
                    exp_scores = jnp.exp2(dot(keys[...], query, 1, 1) * (score_scale * log2_e))
                    prob_grad = dot(values[...], grad, 1, 1)
                    probs = exp_scores * (1.0 / jnp.sum(exp_scores, 0, keepdims=True))
                    row_delta = jnp.sum(probs * prob_grad, 0, keepdims=True)
                    sums[1] += dot(probs.astype(bf16), grad)
                    sums[0] += dot((probs * (prob_grad - row_delta)).astype(bf16), query)
                return carry

            lax.fori_loop(0, group // unroll, step, 0)
            scaled = sums[0] * score_scale * gain_ref[...]
            mean = jnp.mean(scaled * key_raw, -1, keepdims=True)
            key_grad = inv_rms * (scaled - key_raw * inv_rms * inv_rms * mean)
            grads[:, lanes] = key_grad.astype(bf16)
            grads[:, columns + head * head_size : columns + (head + 1) * head_size] = sums[1].astype(bf16)

        for copy in sum(all_weight_copies[1:], []):
            copy.wait()
        for i in range(2):
            here = (table[slices + 2 * blocks] + i) % 2 * half
            turned[i * half : (i + 1) * half, :] = grads[pl.ds(pl.multiple_of(here, half), half), :]

        def token_step(i, carry):
            here = pl.ds(pl.multiple_of(i * lines, lines), lines)
            other_place = pl.multiple_of(table[slices + i] * lines, lines)
            own_place = pl.multiple_of(table[slices + blocks + i] * lines, lines)
            term = dot(weights[0, here, :], turned[:, :columns], 1, 1)
            term += dot(weights[1, here, :], turned[:, columns:], 1, 1)
            own_terms[pl.ds(own_place, lines), :] = term[:, :half].astype(bf16)
            other_terms[pl.ds(other_place, lines), :] = term[:, half:].astype(bf16)
            return carry

        lax.fori_loop(0, blocks, token_step, 0, unroll=4)

    return pl.pallas_call(
        kernel,
        in_specs=[in_smem] + [in_vmem] * 3 + [in_hbm] * 4,
        out_specs=[in_vmem] * 3,
        out_shape=[jax.ShapeDtypeStruct((vis_rows, 2 * columns), bf16)]
        + [jax.ShapeDtypeStruct((depth, half), bf16)] * 2,
        scratch_shapes=[
            pltpu.VMEM((2, depth, columns), bf16),
            pltpu.VMEM((kv_heads, text_rows, group_width), bf16),
            pltpu.VMEM((kv_heads, text_rows, group_width), bf16),
            pltpu.VMEM((vis_rows, head_size), bf16),
            pltpu.VMEM((vis_rows, head_size), bf16),
            pltpu.VMEM((2, vis_rows, head_size), f32),
            pltpu.VMEM((vis_rows, 2 * columns), bf16),
            pltpu.SemaphoreType.DMA((kv_heads, 2)),
            pltpu.SemaphoreType.DMA((slices, 2)),
        ],
        compiler_params=large_params,
        name="middle",
    )(table, last_slice, raw, gain, *map(far_away, (queries, masked, key_proj, value_proj)))


def add_terms(own_terms, core_terms):
    rows, tokens = own_terms.shape
    part = rows // 4

    def kernel(own, other, *outs):
        for i, out in enumerate(outs):
            lines = slice(i * part, (i + 1) * part)
            out[...] = (own[lines, :].astype(f32) + other[lines, :].astype(f32)).astype(bf16)

    return pl.pallas_call(
        kernel,
        in_specs=[in_vmem] * 2,
        out_specs=[in_vmem] * 4,
        out_shape=[jax.ShapeDtypeStruct((part, tokens), bf16)] * 4,
        compiler_params=params,
        name="add_terms",
    )(own_terms, core_terms)


def weight_grads(gathered, own_place, visions, grads):
    width = visions[0].shape[1]
    rows = gathered[0].shape[0]
    columns = grads[0].shape[1] // 2
    steps = 4
    block = width // steps
    count = len(visions)

    def kernel(table, *refs):
        own, others, grad_refs = refs[:4], refs[4 : 4 + count], refs[4 + count : 5 + 2 * count]
        key_out, value_out, picked = refs[-3:]
        for k in range(4):

            @pl.when(table[0] == k)
            def _():
                picked[...] = own[k][...]

        total = 0.0
        for vision, grad in zip([picked, *others], grad_refs):
            total += dot(vision[...], grad[...], 0, 0)
        key_out[...] = total[:, :columns]
        value_out[...] = total[:, columns:]

    return pl.pallas_call(
        kernel,
        grid_spec=pltpu.PrefetchScalarGridSpec(
            num_scalar_prefetch=1,
            grid=(steps,),
            in_specs=[chosen_spec(rows, block, k, 0) for k in range(4)]
            + [pl.BlockSpec((v.shape[0], block), lambda i, table: (0, i)) for v in visions]
            + [pl.BlockSpec(g.shape, lambda i, table: (0, 0)) for g in grads],
            out_specs=[pl.BlockSpec((block, columns), lambda i, table: (i, 0))] * 2,
            scratch_shapes=[pltpu.VMEM((rows, block), bf16)],
        ),
        out_shape=[jax.ShapeDtypeStruct((width, columns), f32)] * 2,
        compiler_params=params,
        name="weight_grads",
    )(own_place, *gathered, *visions, *grads)


def projector_grad(features, others, tokens, dp_place):
    width = others[0].shape[1]
    columns = tokens[0].shape[0]
    steps = 3
    block = width // steps
    count = len(tokens)

    def kernel(place, *refs):
        out = refs[-1]
        total = 0.0
        for feature, token in zip(refs[:count], refs[count : 2 * count]):
            total += dot(feature[...], token[...].astype(f32).T.astype(bf16), 0, 0)
        out[...] = total

    return pl.pallas_call(
        kernel,
        grid_spec=pltpu.PrefetchScalarGridSpec(
            num_scalar_prefetch=1,
            grid=(steps,),
            in_specs=[pl.BlockSpec((features.shape[0], block), lambda i, place: (0, place[0] * steps + i))]
            + [pl.BlockSpec((f.shape[0], block), lambda i, place: (0, i)) for f in others]
            + [pl.BlockSpec(t.shape, lambda i, place: (0, 0)) for t in tokens],
            out_specs=pl.BlockSpec((block, columns), lambda i, place: (i, 0)),
        ),
        out_shape=jax.ShapeDtypeStruct((width, columns), f32),
        compiler_params=params,
        name="projector_grad",
    )(dp_place, features, *others, *tokens)


def int_table(*values):
    return jnp.stack([jnp.asarray(v, jnp.int32) for v in values])


def shards(vision, features, queries, ctx_grad, row_mask, key_weight, value_weight, key_gain):
    z = lax.axis_index("dp")
    pipe = lax.axis_index("pipe")
    tensor = lax.axis_index("tensor")
    y, core = pipe // 2, tensor % 2
    x = (tensor // 2) * 2 + pipe % 2
    key_proj, value_proj = key_weight[0], value_weight[0]
    rows = vision.shape[0]
    half = rows // 2
    dv = features.shape[1] // 4
    near = jnp.where(core == 0, z ^ 1, z ^ 3)

    from_core = send(vision, to_core)
    from_x = send(vision, to_near_x)

    feature_near, feature_far = cut_features(features, int_table(near, z ^ 2, core))
    feature_near = send(feature_near, near_z)
    feature_far = send(feature_far, along_z(2))

    masked = ctx_grad * row_mask[:, None].astype(bf16)
    raw = project([vision, from_core], int_table(tensor, tensor ^ 1), key_proj, value_proj)
    from_x, raw, masked, feature_near, feature_far = lax.optimization_barrier(
        (from_x, raw, masked, feature_near, feature_far)
    )
    from_xc = send(from_x, to_core)
    raw = project([from_x], int_table(tensor ^ 2), key_proj, value_proj, raw)
    from_xc, raw = lax.optimization_barrier((from_xc, raw))
    gathered = [vision, from_core, from_x, from_xc]
    vision_near, vision_far = choose(gathered, int_table(near ^ tensor, z ^ 2 ^ tensor, core))
    vision_near = send(vision_near, near_z)

    block = jnp.arange(16, dtype=jnp.int32)
    block_y, block_x = block // 4, (block % 2) * 2 + block // 2 % 2

    def order(this_core):
        across_x, across_y = block_x ^ x, block_y ^ y
        return jnp.where(this_core == 0, across_x * 4 + across_y, across_y * 4 + across_x)

    table = jnp.concatenate(
        [
            int_table(tensor ^ 3, tensor, tensor ^ 1, tensor ^ 2),
            order(1 - core).astype(jnp.int32),
            order(core).astype(jnp.int32),
            int_table(core),
        ]
    )
    grads, other_terms, own_terms = middle(
        from_xc, raw, queries, masked, key_gain, key_proj, value_proj, table
    )
    grads, other_terms, own_terms, vision_near = lax.optimization_barrier(
        (grads, other_terms, own_terms, vision_near)
    )
    core_terms = send(other_terms, to_core)
    terms = add_terms(own_terms, core_terms)
    terms, vision_near, vision_far, grads, feature_near, feature_far = lax.optimization_barrier(
        (terms, vision_near, vision_far, grads, feature_near, feature_far)
    )
    terms = [term.reshape(4, -1, half) for term in terms]
    arrived = [send(terms[i], first_stage(i)) for i in (1, 2, 3)]
    vision_far = send(vision_far, along_z(2))
    grads_z = [send(grads, along_z(i)) for i in (1, 2, 3)]
    vision_pair = send(vision_near, to_core)
    feature_pair = send(feature_near, to_core)
    feature_far_pair = send(feature_far, to_core)
    arrived, vision_far, vision_pair, feature_pair, feature_far_pair = lax.optimization_barrier(
        (arrived, vision_far, vision_pair, feature_pair, feature_far_pair)
    )
    vision_far_pair = send(vision_far, to_core)
    partial = sum([a.astype(f32) for a in arrived], terms[0].astype(f32))
    partial_bf = partial.astype(bf16)
    arrived = [send(partial_bf[i], second_stage(i)) for i in (1, 2, 3)]
    arrived, grads_z, vision_far_pair = lax.optimization_barrier((arrived, grads_z, vision_far_pair))
    token = sum([a.astype(f32) for a in arrived], partial[0]).astype(bf16)
    token = token.reshape(2, -1, half)
    mine = lax.dynamic_index_in_dim(token, core, 0, False)
    partner = send(lax.dynamic_index_in_dim(token, 1 - core, 0, False), to_core)
    token = jnp.where(
        core == 0, jnp.concatenate([mine, partner], 1), jnp.concatenate([partner, mine], 1)
    )
    tokens_z = [send(token, along_z(i)) for i in (1, 2, 3)]

    def ordered(own, by_z, axis):
        near_one = jnp.where(core == 0, by_z[0], by_z[2])
        near_two = jnp.where(core == 0, by_z[2], by_z[0])
        far_own = lax.dynamic_slice_in_dim(by_z[1], core * half, half, axis)
        far_other = lax.dynamic_slice_in_dim(by_z[1], (1 - core) * half, half, axis)
        return [own, near_one, near_two, jnp.concatenate([far_own, far_other], axis)]

    key_total, value_total = weight_grads(
        gathered,
        int_table(z ^ tensor),
        [vision_near, vision_pair, jnp.concatenate([vision_far, vision_far_pair], 0)],
        ordered(grads, grads_z, 0),
    )
    tokens_z, key_total, value_total = lax.optimization_barrier((tokens_z, key_total, value_total))
    projector_total = projector_grad(
        features,
        [feature_near, feature_pair, jnp.concatenate([feature_far, feature_far_pair], 0)],
        ordered(token, tokens_z, 1),
        int_table(z),
    )
    return (key_total[None], value_total[None], projector_total)


def solution(mesh):
    in_specs = (
        P("dp", "tensor"),
        P("dp", None),
        P("dp", "tensor"),
        P("dp", "tensor"),
        P("dp"),
        P("pipe", None, "tensor"),
        P("pipe", None, "tensor"),
        P("pipe", None),
    )
    out_specs = (P("pipe", "dp", "tensor"), P("pipe", "dp", "tensor"), P("dp", ("pipe", "tensor")))
    return jax.shard_map(shards, mesh=mesh, in_specs=in_specs, out_specs=out_specs, check_vma=False)
```

```python
import jax
import jax.numpy as jnp
from jax import lax
from jax.experimental import pallas as pl
from jax.experimental.pallas import tpu as pltpu
from jax.sharding import PartitionSpec as P

norm_eps = 1e-05
every_axis = ("dp", "pipe", "tensor")
bf16 = jnp.bfloat16
f32 = jnp.float32
head_size = 128
score_scale = head_size**-0.5
log2_e = 1.4426950408889634
megabyte = 2**20


def flat_index(z, y, x, core):
    return z * 32 + y * 8 + (x & 1) * 4 + (x >> 1) * 2 + core


def exchange_pairs(moved):
    pairs = []
    for z in range(4):
        for y in range(4):
            for x in range(4):
                for core in range(2):
                    target = moved(z, y, x, core)
                    if target is not None:
                        pairs.append((flat_index(z, y, x, core), flat_index(*target)))
    return pairs


def send(array, moved):
    return lax.ppermute(array, every_axis, exchange_pairs(moved))


def to_core(z, y, x, core):
    return z, y, x, 1 - core


def to_near_x(z, y, x, core):
    return z, y, x ^ 3, core


def first_stage(k):
    return lambda z, y, x, core: (z, y, x ^ k, core) if core == 0 else (z, y ^ k, x, core)


def second_stage(k):
    return lambda z, y, x, core: (z, y ^ k, x, core) if core == 0 else (z, y, x ^ k, core)


def along_z(k):
    return lambda z, y, x, core: (z ^ k, y, x, core)


def near_z(z, y, x, core):
    return (z ^ 1 if core == 0 else z ^ 3), y, x, core


def vision_near(k):
    return lambda z, y, x, core: None if core == z % 2 else (z ^ k, y, x, core)


def vision_far(z, y, x, core):
    return (z ^ 2, y, x, 1 - core) if core == z % 2 else None


def to_near_y(z, y, x, core):
    return z, y ^ 1, x, core


params = pltpu.CompilerParams(vmem_limit_bytes=14 * megabyte)
small_params = pltpu.CompilerParams(vmem_limit_bytes=4 * megabyte)
large_params = pltpu.CompilerParams(vmem_limit_bytes=26 * megabyte)
def dot(left, right, left_dim=1, right_dim=0):
    return lax.dot_general(
        left, right, (((left_dim,), (right_dim,)), ((), ())), preferred_element_type=f32
    )


at_near, at_far, at_quarter, at_tensor, at_swapped, at_z, at_core = 0, 1, 2, 3, 7, 8, 9
at_own, at_on_parity, at_row_parity, at_other_order, at_own_order = 10, 11, 12, 13, 29

in_vmem = pl.BlockSpec(memory_space=pltpu.VMEM)
in_smem = pl.BlockSpec(memory_space=pltpu.SMEM)


in_hbm = pl.BlockSpec(memory_space=pltpu.HBM)
anywhere = pl.BlockSpec(memory_space=pl.ANY)


def far_away(array):
    return pltpu.with_memory_space_constraint(array, pltpu.HBM)


def chosen_spec(rows, columns, k, place):
    return pl.BlockSpec(
        (rows, columns), lambda i, table: (0, jnp.where(table[place] == k, i, 0))
    )


token_shape = jax.ShapeDtypeStruct((8, 128), f32)


def cut_features(features, table):
    rows, width = features.shape
    width //= 4
    quarter = rows // 4

    def kernel(table, source, near, far, sems):
        def columns(k):
            return pl.ds(pl.multiple_of(table[k] * width, 128), width)

        lines = pl.ds(pl.multiple_of(table[at_quarter] * quarter, quarter), quarter)
        copies = [
            pltpu.make_async_copy(source.at[lines, columns(at_far)], far, sems.at[0]),
            pltpu.make_async_copy(source.at[:, columns(at_near)], near, sems.at[1]),
        ]
        for copy in copies:
            copy.start()
        for copy in copies:
            copy.wait()

    return pl.pallas_call(
        kernel,
        in_specs=[in_smem, in_hbm],
        out_specs=[in_vmem] * 2,
        out_shape=[jax.ShapeDtypeStruct((r, width), bf16) for r in (rows, quarter)],
        scratch_shapes=[pltpu.SemaphoreType.DMA((2,))],
        compiler_params=small_params,
        name="cut_features",
    )(table, far_away(features))


def mask_rows(ctx_grad, mask):
    def kernel(grad_ref, mask_ref, out):
        out[...] = grad_ref[...] * mask_ref[...].astype(bf16)

    rows, width = ctx_grad.shape
    block = pl.BlockSpec((rows, width // 4), lambda i: (0, i))
    return pl.pallas_call(
        kernel,
        grid=(4,),
        in_specs=[block, pl.BlockSpec((rows, 1), lambda i: (0, 0))],
        out_specs=block,
        out_shape=jax.ShapeDtypeStruct(ctx_grad.shape, bf16),
        compiler_params=small_params,
        name="mask_rows",
    )(ctx_grad, mask)


def project(slices, table, key_proj, value_proj):
    rows, width = slices[0].shape
    columns = key_proj.shape[1]
    n = len(slices)

    def kernel(table, *refs):
        slice_refs, projections, (out, done, held, sems) = refs[:n], refs[n : n + 2], refs[n + 2 :]
        done[...] = jnp.zeros_like(done)
        copies = []
        for i in range(n):
            lines = pl.ds(pl.multiple_of(table[at_tensor + i] * width, width), width)
            for j in range(2):
                copy = pltpu.make_async_copy(projections[j].at[lines, :], held.at[i, j], sems.at[i, j])
                copy.start()
                copies.append(copy)
        for j in range(2):
            total = 0.0
            for i in range(n):
                copies[2 * i + j].wait()
                total += dot(slice_refs[i][...], held[i, j])
            out[:, j * columns : (j + 1) * columns] = total

    return pl.pallas_call(
        kernel,
        in_specs=[in_smem] + [in_vmem] * n + [in_hbm] * 2,
        out_specs=[in_vmem] * 2,
        out_shape=[jax.ShapeDtypeStruct((rows, 2 * columns), f32), token_shape],
        scratch_shapes=[pltpu.VMEM((n, 2, width, columns), bf16), pltpu.SemaphoreType.DMA((n, 2))],
        compiler_params=params,
        name="project",
    )(table, *slices, far_away(key_proj), far_away(value_proj))


def choose(own, other, table, after):
    def kernel(table, first, second, *rest):
        one, two, sems = rest[-3:]
        for k, pair in enumerate(((first, second), (second, first))):

            @pl.when(table[at_swapped] == k)
            def _():
                copies = [
                    pltpu.make_async_copy(source, target, sems.at[i])
                    for i, (source, target) in enumerate(zip(pair, (one, two)))
                ]
                for copy in copies:
                    copy.start()
                for copy in copies:
                    copy.wait()

    return pl.pallas_call(
        kernel,
        in_specs=[in_smem] + [in_vmem] * 2 + [anywhere] * len(after),
        out_specs=[in_hbm] * 2,
        out_shape=[pltpu.HBM(own.shape, bf16)] * 2,
        scratch_shapes=[pltpu.SemaphoreType.DMA((2,))],
        compiler_params=small_params,
        name="choose",
    )(table, own, other, *after)


def middle(last_slices, raw, queries, masked, gain, key_proj, value_proj, table):
    vis_rows, width = last_slices[0].shape
    depth, columns = key_proj.shape
    kv_heads = columns // head_size
    text_rows = queries.shape[0]
    group = queries.shape[1] // head_size // kv_heads
    group_width = group * head_size
    half = vis_rows // 2
    blocks = 16
    lines = depth // blocks
    unroll = 4

    def kernel(
        table, slice_one, slice_two, raw_ref, gain_ref, query_ref, masked_ref, key_ref, value_ref,
        grads, other_terms, own_terms,
        keys, values, sums, turned,
    ):
        projected = [raw_ref[:, :columns], raw_ref[:, columns:]]
        for i, slice_ref in enumerate((slice_one, slice_two)):
            place = pl.ds(pl.multiple_of(table[at_tensor + 2 + i] * width, width), width)
            projected[0] += dot(slice_ref[...], key_ref[place, :])
            projected[1] += dot(slice_ref[...], value_ref[place, :])
        key_all, value_all = projected[0], projected[1].astype(bf16)
        for head in range(kv_heads):
            lanes = slice(head * head_size, (head + 1) * head_size)
            key_raw = key_all[:, lanes]
            inv_rms = lax.rsqrt(jnp.mean(key_raw * key_raw, -1, keepdims=True) + norm_eps)
            keys[...] = (key_raw * inv_rms * gain_ref[...]).astype(bf16)
            values[...] = value_all[:, lanes]
            sums[...] = jnp.zeros_like(sums)
            def step(i, carry):
                for j in range(unroll):
                    text = (head * group + i * unroll + j) * head_size
                    text = pl.ds(pl.multiple_of(text, head_size), head_size)
                    query = query_ref[:, text]
                    grad = masked_ref[:, text]
                    exp_scores = jnp.exp2(dot(keys[...], query, 1, 1) * (score_scale * log2_e))
                    prob_grad = dot(values[...], grad, 1, 1)
                    probs = exp_scores * (1.0 / jnp.sum(exp_scores, 0, keepdims=True))
                    row_delta = jnp.sum(probs * prob_grad, 0, keepdims=True)
                    sums[1] += dot(probs.astype(bf16), grad)
                    sums[0] += dot((probs * (prob_grad - row_delta)).astype(bf16), query)
                return carry

            lax.fori_loop(0, group // unroll, step, 0)
            scaled = sums[0] * score_scale * gain_ref[...]
            mean = jnp.mean(scaled * key_raw, -1, keepdims=True)
            key_grad = inv_rms * (scaled - key_raw * inv_rms * inv_rms * mean)
            grads[:, lanes] = key_grad.astype(bf16)
            grads[:, columns + head * head_size : columns + (head + 1) * head_size] = sums[1].astype(bf16)

        for i in range(2):
            here = (table[at_core] + i) % 2 * half
            turned[i * half : (i + 1) * half, :] = grads[pl.ds(pl.multiple_of(here, half), half), :]

        def token_step(i, carry):
            here = pl.ds(pl.multiple_of(i * lines, lines), lines)
            other_place = pl.multiple_of(table[at_other_order + i] * lines, lines)
            own_place = pl.multiple_of(table[at_own_order + i] * lines, lines)
            term = dot(key_ref[here, :], turned[:, :columns], 1, 1)
            term += dot(value_ref[here, :], turned[:, columns:], 1, 1)
            own_terms[pl.ds(own_place, lines), :] = term[:, :half].astype(bf16)
            other_terms[pl.ds(other_place, lines), :] = term[:, half:].astype(bf16)
            return carry

        lax.fori_loop(0, blocks, token_step, 0, unroll=4)

    return pl.pallas_call(
        kernel,
        in_specs=[in_smem] + [in_vmem] * 8,
        out_specs=[in_vmem] * 3,
        out_shape=[jax.ShapeDtypeStruct((vis_rows, 2 * columns), bf16)]
        + [jax.ShapeDtypeStruct((depth, half), bf16)] * 2,
        scratch_shapes=[
            pltpu.VMEM((vis_rows, head_size), bf16),
            pltpu.VMEM((vis_rows, head_size), bf16),
            pltpu.VMEM((2, vis_rows, head_size), f32),
            pltpu.VMEM((vis_rows, 2 * columns), bf16),
        ],
        compiler_params=large_params,
        name="middle",
    )(table, *last_slices, raw, gain, queries, masked, key_proj, value_proj)


def wait_for(array, after):
    return pl.pallas_call(
        lambda *refs: None,
        in_specs=[anywhere] * (1 + len(after)),
        out_specs=anywhere,
        out_shape=jax.ShapeDtypeStruct(array.shape, array.dtype),
        input_output_aliases={0: 0},
        compiler_params=small_params,
        name="wait_for",
    )(array, *after)


def add_terms(own_terms, core_terms, after):
    rows, tokens = own_terms.shape
    part = rows // 4

    def kernel(own, other, *rest):
        for i, out in enumerate(rest[-4:]):
            lines = slice(i * part, (i + 1) * part)
            out[...] = (own[lines, :].astype(f32) + other[lines, :].astype(f32)).astype(bf16)

    return pl.pallas_call(
        kernel,
        in_specs=[in_vmem] * 2 + [anywhere] * len(after),
        out_specs=[in_vmem] * 4,
        out_shape=[jax.ShapeDtypeStruct((part, tokens), bf16)] * 4,
        compiler_params=params,
        name="add_terms",
    )(own_terms, core_terms, *after)


def add_first(parts, after):
    rows, tokens = parts[0].shape
    block = rows // 4

    def kernel(*refs):
        own, *outs = refs[-4:]
        for i, out in enumerate((own, *outs)):
            lines = slice(i * block, (i + 1) * block)
            out[...] = sum(ref[lines, :].astype(f32) for ref in refs[:4]).astype(out.dtype)

    return pl.pallas_call(
        kernel,
        in_specs=[in_vmem] * 4 + [anywhere] * len(after),
        out_specs=[in_vmem] * 4,
        out_shape=[jax.ShapeDtypeStruct((block, tokens), f32)]
        + [jax.ShapeDtypeStruct((block, tokens), bf16)] * 3,
        compiler_params=small_params,
        name="add_first",
    )(*parts, *after)


def add_second(own, arrived, table, after):
    rows, tokens = own.shape
    half = rows // 2

    def kernel(table, *refs):
        for i, out in enumerate(refs[-2:]):
            lines = pl.ds(pl.multiple_of((table[at_core] + i) % 2 * half, half), half)
            out[...] = sum(ref[lines, :].astype(f32) for ref in refs[:4]).astype(bf16)

    return pl.pallas_call(
        kernel,
        in_specs=[in_smem] + [in_vmem] * 4 + [anywhere] * len(after),
        out_specs=[in_vmem] * 2,
        out_shape=[jax.ShapeDtypeStruct((half, tokens), bf16)] * 2,
        compiler_params=small_params,
        name="add_second",
    )(table, own, *arrived, *after)


def weight_grads(gathered, by_z, pairs, table, grads, after):
    rows, width = gathered[0].shape
    columns = grads[0].shape[1] // 2
    steps = 4
    block = width // steps
    choices = [[(at_own, k, v) for k, v in enumerate(gathered)]]
    choices += [
        [(at_on_parity, int(i < 2), by_z[i]), (at_on_parity, int(i == 2), pairs[i])] for i in range(3)
    ]
    flat = sum(choices, [])

    def kernel(table, *refs):
        vision_refs, grad_refs, (key_out, value_out, done, picked) = refs[: len(flat)], refs[len(flat) : -5], refs[-4:]
        done[...] = jnp.zeros_like(done)
        total = 0.0
        at = 0
        for i, options in enumerate(choices):
            for place, value, _ in options:

                @pl.when(table[place] == value)
                def _(ref=vision_refs[at]):
                    picked[i] = ref[...]

                at += 1
        for i in range(4):
            total += dot(picked[i], grad_refs[i][...], 0, 0)
        key_out[...] = total[:, :columns]
        value_out[...] = total[:, columns:]

    return pl.pallas_call(
        kernel,
        grid_spec=pltpu.PrefetchScalarGridSpec(
            num_scalar_prefetch=1,
            grid=(steps,),
            in_specs=[chosen_spec(rows, block, value, place) for place, value, _ in flat]
            + [pl.BlockSpec(g.shape, lambda i, table: (0, 0)) for g in grads]
            + [anywhere],
            out_specs=[pl.BlockSpec((block, columns), lambda i, table: (i, 0))] * 2
            + [pl.BlockSpec(token_shape.shape, lambda i, table: (0, 0))],
            scratch_shapes=[pltpu.VMEM((4, rows, block), bf16)],
        ),
        out_shape=[jax.ShapeDtypeStruct((width, columns), f32)] * 2 + [token_shape],
        compiler_params=params,
        name="weight_grads",
    )(table, *[v for _, _, v in flat], *grads, after)


def join_tokens(mine, partner, table):
    rows, half = mine.shape

    def kernel(table, one, two, out):
        for k, pair in enumerate(((one, two), (two, one))):

            @pl.when(table[at_core] == k)
            def _():
                for i, ref in enumerate(pair):
                    out[:, i * half : (i + 1) * half] = ref[...]

    return pl.pallas_call(
        kernel,
        in_specs=[in_smem] + [in_vmem] * 2,
        out_specs=in_vmem,
        out_shape=jax.ShapeDtypeStruct((rows, 2 * half), bf16),
        compiler_params=small_params,
        name="join_tokens",
    )(table, mine, partner)


def turn_features(features, near, near_pair, far, table, after):
    rows, width = near.shape
    quarter = rows // 4
    steps = 3
    block = width // steps

    def kernel(table, own_ref, near_ref, near_pair_ref, *rest):
        out, done, joined = rest[-3:]
        done[...] = jnp.zeros_like(done)
        for i, ref in enumerate(rest[:4]):
            place = (table[at_core] + i // 2) % 2 * 2 + (table[at_row_parity] + i % 2) % 2
            joined[pl.ds(pl.multiple_of(place * quarter, quarter), quarter), :] = ref[...]
        for i, ref in enumerate((own_ref, near_ref, near_pair_ref, joined)):
            out[:, i * rows : (i + 1) * rows] = ref[...].T

    return pl.pallas_call(
        kernel,
        grid_spec=pltpu.PrefetchScalarGridSpec(
            num_scalar_prefetch=1,
            grid=(steps,),
            in_specs=[pl.BlockSpec((rows, block), lambda i, table: (0, table[at_z] * steps + i))]
            + [pl.BlockSpec((rows, block), lambda i, table: (0, i))] * 2
            + [pl.BlockSpec((quarter, block), lambda i, table: (0, i))] * 4
            + [anywhere],
            out_specs=[
                pl.BlockSpec((block, 4 * rows), lambda i, table: (i, 0)),
                pl.BlockSpec(token_shape.shape, lambda i, table: (0, 0)),
            ],
            scratch_shapes=[pltpu.VMEM((rows, block), bf16)],
        ),
        out_shape=[jax.ShapeDtypeStruct((width, 4 * rows), bf16), token_shape],
        compiler_params=params,
        name="turn_features",
    )(table, far_away(features), near, near_pair, *far, after)


def projector_grad(turned, token, tokens_z, table, after):
    width, depth = turned.shape
    columns = token.shape[0]
    rows = depth // 4
    steps = 3
    block = width // steps

    def kernel(table, feature_ref, *refs):
        out, near = refs[-2:]
        for k, pair in enumerate(((1, 3), (3, 1))):

            @pl.when(table[at_core] == k)
            def _():
                for i in range(2):
                    near[i] = refs[pair[i]][...]

        total = 0.0
        for i, term in enumerate((refs[0][...], near[0], near[1], refs[2][...])):
            total += dot(feature_ref[:, i * rows : (i + 1) * rows], term, 1, 1)
        out[...] = total

    return pl.pallas_call(
        kernel,
        grid_spec=pltpu.PrefetchScalarGridSpec(
            num_scalar_prefetch=1,
            grid=(steps,),
            in_specs=[pl.BlockSpec((block, depth), lambda i, table: (i, 0))]
            + [pl.BlockSpec(token.shape, lambda i, table: (0, 0))] * 4
            + [anywhere],
            out_specs=pl.BlockSpec((block, columns), lambda i, table: (i, 0)),
            scratch_shapes=[pltpu.VMEM((2, *token.shape), bf16)],
        ),
        out_shape=jax.ShapeDtypeStruct((width, columns), f32),
        compiler_params=params,
        name="projector_grad",
    )(table, turned, token, *tokens_z, after)


def integers(z, pipe, tensor):
    y, core = pipe // 2, tensor % 2
    x = (tensor // 2) * 2 + pipe % 2
    on_parity = (core == z % 2).astype(jnp.int32)
    values = [jnp.where(core == 0, z ^ 1, z ^ 3), z ^ 2, 2 * core + y % 2]
    values += [tensor, tensor ^ 1, tensor ^ 2, tensor ^ 3]
    values += [(tensor // 2 == z // 2).astype(jnp.int32) ^ (1 - on_parity), z, core]
    values += [z ^ tensor, on_parity, y % 2]
    for this_core in (1 - core, core):
        for block in range(16):
            across_y, across_x = y ^ (block // 4), x ^ (block % 2 * 2 + block // 2 % 2)
            values.append(
                jnp.where(this_core == 0, across_x * 4 + across_y, across_y * 4 + across_x)
            )
    return jnp.stack(values).astype(jnp.int32)


def shards(vision, features, queries, ctx_grad, row_mask, key_weight, value_weight, key_gain):
    key_proj, value_proj = key_weight[0], value_weight[0]
    table = integers(lax.axis_index("dp"), lax.axis_index("pipe"), lax.axis_index("tensor"))

    from_core = send(vision, to_core)
    from_x = send(vision, to_near_x)

    feature_near, feature_far = cut_features(features, table)
    feature_near = send(feature_near, near_z)
    feature_far = send(feature_far, along_z(2))

    masked = mask_rows(ctx_grad, row_mask[:, None])
    raw, done = project([vision, from_core], table, key_proj, value_proj)
    from_x = wait_for(from_x, [done, masked, feature_near, feature_far])
    from_xc = send(from_x, to_core)
    vision_one, vision_two = choose(vision, from_x, table, [])
    gathered = [vision, from_core, from_x, from_xc]
    by_z = [send(vision_one, vision_near(1)), send(vision_two, vision_near(3))]
    feature_far = [feature_far, send(feature_far, to_near_y)]
    grads, other_terms, own_terms = middle(
        [from_x, from_xc], raw, queries, masked, key_gain, key_proj, value_proj, table
    )

    core_terms = send(wait_for(other_terms, by_z + feature_far), to_core)
    by_z.append(send(vision_one, vision_far))
    feature_far += [send(part, to_core) for part in feature_far]
    terms = add_terms(own_terms, core_terms, feature_far)
    arrived = [send(terms[i], first_stage(i)) for i in (1, 2, 3)]
    feature_near = wait_for(feature_near, [terms[0]])
    feature_pair = send(feature_near, to_core)
    own, *partial = add_first([terms[0], *arrived], [by_z[2], feature_pair])
    grads = wait_for(grads, [own])
    grads_z = {i: send(grads, along_z(i)) for i in (1, 2, 3)}
    arrived = [send(partial[i - 1], second_stage(i)) for i in (1, 2, 3)]
    turned, done = turn_features(features, feature_near, feature_pair, feature_far, table, own)
    mine, other = add_second(own, arrived, table, [done, *grads_z.values()])
    token = join_tokens(mine, send(other, to_core), table)
    tokens_z = [send(token, along_z(i)) for i in (1, 2, 3)]

    by_z = [wait_for(array, [token]) for array in by_z]
    pairs = [send(array, to_core) for array in by_z]
    key_total, value_total, done = weight_grads(
        gathered, by_z, pairs, table, [grads, *(grads_z[i] for i in (1, 3, 2))], token
    )
    projector_total = projector_grad(turned, token, tokens_z, table, done)
    return (key_total[None], value_total[None], projector_total)


def solution(mesh):
    in_specs = (
        P("dp", "tensor"),
        P("dp", None),
        P("dp", "tensor"),
        P("dp", "tensor"),
        P("dp"),
        P("pipe", None, "tensor"),
        P("pipe", None, "tensor"),
        P("pipe", None),
    )
    out_specs = (P("pipe", "dp", "tensor"), P("pipe", "dp", "tensor"), P("dp", ("pipe", "tensor")))
    return jax.shard_map(shards, mesh=mesh, in_specs=in_specs, out_specs=out_specs, check_vma=False)
```

```python
import jax
import jax.numpy as jnp
from jax import lax
from jax.experimental import pallas as pl
from jax.experimental.pallas import tpu as pltpu
from jax.sharding import PartitionSpec as P

norm_eps = 1e-05
every_axis = ("dp", "pipe", "tensor")
bf16 = jnp.bfloat16
f32 = jnp.float32
head_size = 128
score_scale = head_size**-0.5
log2_e = 1.4426950408889634
megabyte = 2**20


def flat_index(z, y, x, core):
    return z * 32 + y * 8 + (x & 1) * 4 + (x >> 1) * 2 + core


def exchange_pairs(moved):
    pairs = []
    for z in range(4):
        for y in range(4):
            for x in range(4):
                for core in range(2):
                    target = moved(z, y, x, core)
                    if target is not None:
                        pairs.append((flat_index(z, y, x, core), flat_index(*target)))
    return pairs


def send(array, moved):
    return lax.ppermute(array, every_axis, exchange_pairs(moved))


def to_core(z, y, x, core):
    return z, y, x, 1 - core


def to_near_x(z, y, x, core):
    return z, y, x ^ 3, core


def first_stage(k):
    return lambda z, y, x, core: (z, y, x ^ k, core) if core == 0 else (z, y ^ k, x, core)


def second_stage(k):
    return lambda z, y, x, core: (z, y ^ k, x, core) if core == 0 else (z, y, x ^ k, core)


def along_z(k):
    return lambda z, y, x, core: (z ^ k, y, x, core)


def near_z(z, y, x, core):
    return (z ^ 1 if core == 0 else z ^ 3), y, x, core


def vision_near(k):
    return lambda z, y, x, core: None if core == z % 2 else (z ^ k, y, x, core)


def vision_far(z, y, x, core):
    return (z ^ 2, y, x, 1 - core) if core == z % 2 else None


def to_near_y(z, y, x, core):
    return z, y ^ 1, x, core


params = pltpu.CompilerParams(vmem_limit_bytes=14 * megabyte)
small_params = pltpu.CompilerParams(vmem_limit_bytes=4 * megabyte)
large_params = pltpu.CompilerParams(vmem_limit_bytes=26 * megabyte)
def dot(left, right, left_dim=1, right_dim=0):
    return lax.dot_general(
        left, right, (((left_dim,), (right_dim,)), ((), ())), preferred_element_type=f32
    )


at_near, at_far, at_quarter, at_tensor, at_swapped, at_z, at_core = 0, 1, 2, 3, 7, 8, 9
at_own, at_on_parity, at_row_parity, at_other_order, at_own_order = 10, 11, 12, 13, 29

in_vmem = pl.BlockSpec(memory_space=pltpu.VMEM)
in_smem = pl.BlockSpec(memory_space=pltpu.SMEM)


in_hbm = pl.BlockSpec(memory_space=pltpu.HBM)
anywhere = pl.BlockSpec(memory_space=pl.ANY)


def far_away(array):
    return pltpu.with_memory_space_constraint(array, pltpu.HBM)


def chosen_spec(rows, columns, k, place):
    return pl.BlockSpec(
        (rows, columns), lambda i, table: (0, jnp.where(table[place] == k, i, 0))
    )


token_shape = jax.ShapeDtypeStruct((8, 128), f32)


def cut_features(features, table):
    rows, width = features.shape
    width //= 4
    quarter = rows // 4

    def kernel(table, source, near, far, sems):
        def columns(k):
            return pl.ds(pl.multiple_of(table[k] * width, 128), width)

        lines = pl.ds(pl.multiple_of(table[at_quarter] * quarter, quarter), quarter)
        copies = [
            pltpu.make_async_copy(source.at[lines, columns(at_far)], far, sems.at[0]),
            pltpu.make_async_copy(source.at[:, columns(at_near)], near, sems.at[1]),
        ]
        for copy in copies:
            copy.start()
        for copy in copies:
            copy.wait()

    return pl.pallas_call(
        kernel,
        in_specs=[in_smem, in_hbm],
        out_specs=[in_vmem] * 2,
        out_shape=[jax.ShapeDtypeStruct((r, width), bf16) for r in (rows, quarter)],
        scratch_shapes=[pltpu.SemaphoreType.DMA((2,))],
        compiler_params=small_params,
        name="cut_features",
    )(table, far_away(features))


def mask_rows(ctx_grad, mask):
    def kernel(grad_ref, mask_ref, out):
        out[...] = grad_ref[...] * mask_ref[...].astype(bf16)

    rows, width = ctx_grad.shape
    block = pl.BlockSpec((rows, width // 4), lambda i: (0, i))
    return pl.pallas_call(
        kernel,
        grid=(4,),
        in_specs=[block, pl.BlockSpec((rows, 1), lambda i: (0, 0))],
        out_specs=block,
        out_shape=jax.ShapeDtypeStruct(ctx_grad.shape, bf16),
        compiler_params=small_params,
        name="mask_rows",
    )(ctx_grad, mask)


def project(slices, table, key_proj, value_proj):
    rows, width = slices[0].shape
    columns = key_proj.shape[1]
    n = len(slices)

    def kernel(table, *refs):
        slice_refs, projections, (out, done, held, sems) = refs[:n], refs[n : n + 2], refs[n + 2 :]
        done[...] = jnp.zeros_like(done)
        copies = []
        for i in range(n):
            lines = pl.ds(pl.multiple_of(table[at_tensor + i] * width, width), width)
            for j in range(2):
                copy = pltpu.make_async_copy(projections[j].at[lines, :], held.at[i, j], sems.at[i, j])
                copy.start()
                copies.append(copy)
        for j in range(2):
            total = 0.0
            for i in range(n):
                copies[2 * i + j].wait()
                total += dot(slice_refs[i][...], held[i, j])
            out[:, j * columns : (j + 1) * columns] = total

    return pl.pallas_call(
        kernel,
        in_specs=[in_smem] + [in_vmem] * n + [in_hbm] * 2,
        out_specs=[in_vmem] * 2,
        out_shape=[jax.ShapeDtypeStruct((rows, 2 * columns), f32), token_shape],
        scratch_shapes=[pltpu.VMEM((n, 2, width, columns), bf16), pltpu.SemaphoreType.DMA((n, 2))],
        compiler_params=params,
        name="project",
    )(table, *slices, far_away(key_proj), far_away(value_proj))


def choose(own, other, table):
    def kernel(table, first, second, one, two):
        for k, (a, b) in enumerate(((first, second), (second, first))):

            @pl.when(table[at_swapped] == k)
            def _():
                one[...] = a[...]
                two[...] = b[...]

    return pl.pallas_call(
        kernel,
        in_specs=[in_smem] + [in_vmem] * 2,
        out_specs=[in_vmem] * 2,
        out_shape=[jax.ShapeDtypeStruct(own.shape, bf16)] * 2,
        compiler_params=small_params,
        name="choose",
    )(table, own, other)


def middle(last_slices, raw, queries, masked, gain, key_proj, value_proj, table):
    vis_rows, width = last_slices[0].shape
    depth, columns = key_proj.shape
    kv_heads = columns // head_size
    text_rows = queries.shape[0]
    group = queries.shape[1] // head_size // kv_heads
    group_width = group * head_size
    half = vis_rows // 2
    blocks = 16
    lines = depth // blocks
    unroll = 8

    def kernel(
        table, slice_one, slice_two, raw_ref, gain_ref, query_ref, masked_ref, key_ref, value_ref,
        grads, other_terms, own_terms,
        keys, values, sums, turned,
    ):
        projected = [raw_ref[:, :columns], raw_ref[:, columns:]]
        for i, slice_ref in enumerate((slice_one, slice_two)):
            place = pl.ds(pl.multiple_of(table[at_tensor + 2 + i] * width, width), width)
            projected[0] += dot(slice_ref[...], key_ref[place, :])
            projected[1] += dot(slice_ref[...], value_ref[place, :])
        key_all, value_all = projected[0], projected[1].astype(bf16)
        for head in range(kv_heads):
            lanes = slice(head * head_size, (head + 1) * head_size)
            key_raw = key_all[:, lanes]
            inv_rms = lax.rsqrt(jnp.mean(key_raw * key_raw, -1, keepdims=True) + norm_eps)
            keys[...] = (key_raw * inv_rms * gain_ref[...]).astype(bf16)
            values[...] = value_all[:, lanes]
            sums[...] = jnp.zeros_like(sums)
            def step(i, carry):
                for j in range(unroll):
                    text = (head * group + i * unroll + j) * head_size
                    text = pl.ds(pl.multiple_of(text, head_size), head_size)
                    query = query_ref[:, text]
                    grad = masked_ref[:, text]
                    exp_scores = jnp.exp2(dot(keys[...], query, 1, 1) * (score_scale * log2_e))
                    prob_grad = dot(values[...], grad, 1, 1)
                    probs = exp_scores * (1.0 / jnp.sum(exp_scores, 0, keepdims=True))
                    row_delta = jnp.sum(probs * prob_grad, 0, keepdims=True)
                    sums[1] += dot(probs.astype(bf16), grad)
                    sums[0] += dot((probs * (prob_grad - row_delta)).astype(bf16), query)
                return carry

            lax.fori_loop(0, group // unroll, step, 0)
            scaled = sums[0] * score_scale * gain_ref[...]
            mean = jnp.mean(scaled * key_raw, -1, keepdims=True)
            key_grad = inv_rms * (scaled - key_raw * inv_rms * inv_rms * mean)
            grads[:, lanes] = key_grad.astype(bf16)
            grads[:, columns + head * head_size : columns + (head + 1) * head_size] = sums[1].astype(bf16)

        for i in range(2):
            here = (table[at_core] + i) % 2 * half
            turned[i * half : (i + 1) * half, :] = grads[pl.ds(pl.multiple_of(here, half), half), :]

        def token_step(i, carry):
            here = pl.ds(pl.multiple_of(i * lines, lines), lines)
            other_place = pl.multiple_of(table[at_other_order + i] * lines, lines)
            own_place = pl.multiple_of(table[at_own_order + i] * lines, lines)
            term = dot(key_ref[here, :], turned[:, :columns], 1, 1)
            term += dot(value_ref[here, :], turned[:, columns:], 1, 1)
            own_terms[pl.ds(own_place, lines), :] = term[:, :half].astype(bf16)
            other_terms[pl.ds(other_place, lines), :] = term[:, half:].astype(bf16)
            return carry

        lax.fori_loop(0, blocks, token_step, 0, unroll=4)

    return pl.pallas_call(
        kernel,
        in_specs=[in_smem] + [in_vmem] * 8,
        out_specs=[in_vmem] * 3,
        out_shape=[jax.ShapeDtypeStruct((vis_rows, 2 * columns), bf16)]
        + [jax.ShapeDtypeStruct((depth, half), bf16)] * 2,
        scratch_shapes=[
            pltpu.VMEM((vis_rows, head_size), bf16),
            pltpu.VMEM((vis_rows, head_size), bf16),
            pltpu.VMEM((2, vis_rows, head_size), f32),
            pltpu.VMEM((vis_rows, 2 * columns), bf16),
        ],
        compiler_params=large_params,
        name="middle",
    )(table, *last_slices, raw, gain, queries, masked, key_proj, value_proj)


def wait_for(array, after):
    return pl.pallas_call(
        lambda *refs: None,
        in_specs=[anywhere] * (1 + len(after)),
        out_specs=anywhere,
        out_shape=jax.ShapeDtypeStruct(array.shape, array.dtype),
        input_output_aliases={0: 0},
        compiler_params=small_params,
        name="wait_for",
    )(array, *after)


def add_terms(own_terms, core_terms, after):
    rows, tokens = own_terms.shape
    part = rows // 4

    def kernel(own, other, *rest):
        for i, out in enumerate(rest[-4:]):
            lines = slice(i * part, (i + 1) * part)
            out[...] = (own[lines, :].astype(f32) + other[lines, :].astype(f32)).astype(bf16)

    return pl.pallas_call(
        kernel,
        in_specs=[in_vmem] * 2 + [anywhere] * len(after),
        out_specs=[in_vmem] * 4,
        out_shape=[jax.ShapeDtypeStruct((part, tokens), bf16)] * 4,
        compiler_params=params,
        name="add_terms",
    )(own_terms, core_terms, *after)


def add_first(parts, after):
    rows, tokens = parts[0].shape
    block = rows // 4

    def kernel(*refs):
        own, *outs = refs[-4:]
        for i, out in enumerate((own, *outs)):
            lines = slice(i * block, (i + 1) * block)
            out[...] = sum(ref[lines, :].astype(f32) for ref in refs[:4]).astype(out.dtype)

    return pl.pallas_call(
        kernel,
        in_specs=[in_vmem] * 4 + [anywhere] * len(after),
        out_specs=[in_vmem] * 4,
        out_shape=[jax.ShapeDtypeStruct((block, tokens), f32)]
        + [jax.ShapeDtypeStruct((block, tokens), bf16)] * 3,
        compiler_params=small_params,
        name="add_first",
    )(*parts, *after)


def add_second(own, arrived, table, after):
    rows, tokens = own.shape
    half = rows // 2

    def kernel(table, *refs):
        for i in range(2):
            lines = pl.ds(pl.multiple_of((table[at_core] + i) % 2 * half, half), half)
            total = sum(ref[lines, :].astype(f32) for ref in refs[:4]).astype(bf16)
            refs[-1][i * half : (i + 1) * half, :] = total

    return pl.pallas_call(
        kernel,
        in_specs=[in_smem] + [in_vmem] * 4 + [anywhere] * len(after),
        out_specs=in_vmem,
        out_shape=jax.ShapeDtypeStruct((rows, tokens), bf16),
        compiler_params=small_params,
        name="add_second",
    )(table, own, *arrived, *after)


def weight_grads(gathered, by_z, pairs, table, grads, after):
    rows, width = gathered[0].shape
    columns = grads[0].shape[1] // 2
    steps = 4
    block = width // steps
    choices = [[(at_own, k, v) for k, v in enumerate(gathered)]]
    choices += [
        [(at_on_parity, int(i < 2), by_z[i]), (at_on_parity, int(i == 2), pairs[i])] for i in range(3)
    ]
    flat = sum(choices, [])

    def kernel(table, *refs):
        vision_refs, grad_refs, (key_out, value_out, done, picked) = refs[: len(flat)], refs[len(flat) : -5], refs[-4:]
        done[...] = jnp.zeros_like(done)
        total = 0.0
        at = 0
        for i, options in enumerate(choices):
            for place, value, _ in options:

                @pl.when(table[place] == value)
                def _(ref=vision_refs[at]):
                    picked[i] = ref[...]

                at += 1
        for i in range(4):
            total += dot(picked[i], grad_refs[i][...], 0, 0)
        key_out[...] = total[:, :columns]
        value_out[...] = total[:, columns:]

    return pl.pallas_call(
        kernel,
        grid_spec=pltpu.PrefetchScalarGridSpec(
            num_scalar_prefetch=1,
            grid=(steps,),
            in_specs=[chosen_spec(rows, block, value, place) for place, value, _ in flat]
            + [pl.BlockSpec(g.shape, lambda i, table: (0, 0)) for g in grads]
            + [anywhere],
            out_specs=[pl.BlockSpec((block, columns), lambda i, table: (i, 0))] * 2
            + [pl.BlockSpec(token_shape.shape, lambda i, table: (0, 0))],
            scratch_shapes=[pltpu.VMEM((4, rows, block), bf16)],
        ),
        out_shape=[jax.ShapeDtypeStruct((width, columns), f32)] * 2 + [token_shape],
        compiler_params=params,
        name="weight_grads",
    )(table, *[v for _, _, v in flat], *grads, after)


def turn_features(features, near, near_pair, far, table, after):
    rows, width = near.shape
    quarter = rows // 4
    steps = 3
    block = width // steps

    def kernel(table, own_ref, near_ref, near_pair_ref, *rest):
        out, done, joined = rest[-3:]
        done[...] = jnp.zeros_like(done)
        for i, ref in enumerate(rest[:4]):
            place = (table[at_core] + i // 2) % 2 * 2 + (table[at_row_parity] + i % 2) % 2
            joined[pl.ds(pl.multiple_of(place * quarter, quarter), quarter), :] = ref[...]
        for i, ref in enumerate((own_ref, near_ref, near_pair_ref, joined)):
            out[:, i * rows : (i + 1) * rows] = ref[...].T

    return pl.pallas_call(
        kernel,
        grid_spec=pltpu.PrefetchScalarGridSpec(
            num_scalar_prefetch=1,
            grid=(steps,),
            in_specs=[pl.BlockSpec((rows, block), lambda i, table: (0, table[at_z] * steps + i))]
            + [pl.BlockSpec((rows, block), lambda i, table: (0, i))] * 2
            + [pl.BlockSpec((quarter, block), lambda i, table: (0, i))] * 4
            + [anywhere],
            out_specs=[
                pl.BlockSpec((block, 4 * rows), lambda i, table: (i, 0)),
                pl.BlockSpec(token_shape.shape, lambda i, table: (0, 0)),
            ],
            scratch_shapes=[pltpu.VMEM((rows, block), bf16)],
        ),
        out_shape=[jax.ShapeDtypeStruct((width, 4 * rows), bf16), token_shape],
        compiler_params=params,
        name="turn_features",
    )(table, far_away(features), near, near_pair, *far, after)


def projector_grad(turned, tokens, partners, table, after):
    width, depth = turned.shape
    rows, half = tokens[0].shape
    columns = rows // 2
    steps = 3
    block = width // steps

    def kernel(table, feature_ref, *refs):
        out, joined = refs[-2:]
        for k in range(2):

            @pl.when(table[at_core] == k)
            def _():
                for i, image in enumerate((0, 1, 3, 2) if k == 0 else (0, 3, 1, 2)):
                    joined[i, :, k * half : (k + 1) * half] = refs[image][:columns, :]
                    joined[i, :, (1 - k) * half : (2 - k) * half] = refs[4 + image][columns:, :]

        total = 0.0
        for i in range(4):
            total += dot(feature_ref[:, i * 2 * half : (i + 1) * 2 * half], joined[i], 1, 1)
        out[...] = total

    return pl.pallas_call(
        kernel,
        grid_spec=pltpu.PrefetchScalarGridSpec(
            num_scalar_prefetch=1,
            grid=(steps,),
            in_specs=[pl.BlockSpec((block, depth), lambda i, table: (i, 0))]
            + [pl.BlockSpec((rows, half), lambda i, table: (0, 0))] * 8
            + [anywhere],
            out_specs=pl.BlockSpec((block, columns), lambda i, table: (i, 0)),
            scratch_shapes=[pltpu.VMEM((4, columns, 2 * half), bf16)],
        ),
        out_shape=jax.ShapeDtypeStruct((width, columns), f32),
        compiler_params=params,
        name="projector_grad",
    )(table, turned, *tokens, *partners, after)


def integers(z, pipe, tensor):
    y, core = pipe // 2, tensor % 2
    x = (tensor // 2) * 2 + pipe % 2
    on_parity = (core == z % 2).astype(jnp.int32)
    values = [jnp.where(core == 0, z ^ 1, z ^ 3), z ^ 2, 2 * core + y % 2]
    values += [tensor, tensor ^ 1, tensor ^ 2, tensor ^ 3]
    values += [(tensor // 2 == z // 2).astype(jnp.int32) ^ (1 - on_parity), z, core]
    values += [z ^ tensor, on_parity, y % 2]
    for this_core in (1 - core, core):
        for block in range(16):
            across_y, across_x = y ^ (block // 4), x ^ (block % 2 * 2 + block // 2 % 2)
            values.append(
                jnp.where(this_core == 0, across_x * 4 + across_y, across_y * 4 + across_x)
            )
    return jnp.stack(values).astype(jnp.int32)


def shards(vision, features, queries, ctx_grad, row_mask, key_weight, value_weight, key_gain):
    key_proj, value_proj = key_weight[0], value_weight[0]
    table = integers(lax.axis_index("dp"), lax.axis_index("pipe"), lax.axis_index("tensor"))

    from_core = send(vision, to_core)
    from_x = send(vision, to_near_x)

    feature_near, feature_far = cut_features(features, table)
    feature_near = send(feature_near, near_z)
    feature_far = send(feature_far, along_z(2))

    masked = mask_rows(ctx_grad, row_mask[:, None])
    raw, done = project([vision, from_core], table, key_proj, value_proj)
    from_x = wait_for(from_x, [done, masked, feature_near, feature_far])
    from_xc = send(from_x, to_core)
    vision_one, vision_two = choose(vision, from_x, table)
    gathered = [vision, from_core, from_x, from_xc]
    by_z = [send(vision_one, vision_near(1)), send(vision_two, vision_near(3))]
    feature_far = [feature_far, send(feature_far, to_near_y)]
    grads, other_terms, own_terms = middle(
        [from_x, from_xc], raw, queries, masked, key_gain, key_proj, value_proj, table
    )

    core_terms = send(wait_for(other_terms, by_z + feature_far), to_core)
    by_z.append(send(vision_one, vision_far))
    feature_far += [send(part, to_core) for part in feature_far]
    terms = add_terms(own_terms, core_terms, feature_far)
    arrived = [send(terms[i], first_stage(i)) for i in (1, 2, 3)]
    grads_z = {i: send(grads, along_z(i)) for i in (1, 2, 3)}
    own, *partial = add_first([terms[0], *arrived], [by_z[2], grads_z[2]])
    arrived = [send(partial[i - 1], second_stage(i)) for i in (1, 2, 3)]
    feature_near = wait_for(feature_near, [own])
    feature_pair = send(feature_near, to_core)
    turned, done = turn_features(features, feature_near, feature_pair, feature_far, table, own)
    token = add_second(own, arrived, table, [done, grads_z[1], grads_z[3]])
    tokens = [token, *(send(token, along_z(i)) for i in (1, 2, 3))]
    by_z = [wait_for(array, [token]) for array in by_z]
    pairs = [send(array, to_core) for array in by_z]
    key_total, value_total, done = weight_grads(
        gathered, by_z, pairs, table, [grads, *(grads_z[i] for i in (1, 3, 2))], token
    )
    tokens[1:] = [wait_for(array, [done]) for array in tokens[1:]]
    partners = [send(array, to_core) for array in tokens]
    projector_total = projector_grad(turned, tokens, partners, table, done)
    return (key_total[None], value_total[None], projector_total)


def solution(mesh):
    in_specs = (
        P("dp", "tensor"),
        P("dp", None),
        P("dp", "tensor"),
        P("dp", "tensor"),
        P("dp"),
        P("pipe", None, "tensor"),
        P("pipe", None, "tensor"),
        P("pipe", None),
    )
    out_specs = (P("pipe", "dp", "tensor"), P("pipe", "dp", "tensor"), P("dp", ("pipe", "tensor")))
    return jax.shard_map(shards, mesh=mesh, in_specs=in_specs, out_specs=out_specs, check_vma=False)
```

```python
import jax
import jax.numpy as jnp
from jax import lax
from jax.experimental import pallas as pl
from jax.experimental.pallas import tpu as pltpu
from jax.sharding import PartitionSpec as P

norm_eps = 1e-05
every_axis = ("dp", "pipe", "tensor")
bf16 = jnp.bfloat16
f32 = jnp.float32
head_size = 128
score_scale = head_size**-0.5
log2_e = 1.4426950408889634
megabyte = 2**20


def flat_index(z, y, x, core):
    return z * 32 + y * 8 + (x & 1) * 4 + (x >> 1) * 2 + core


def exchange_pairs(moved):
    pairs = []
    for z in range(4):
        for y in range(4):
            for x in range(4):
                for core in range(2):
                    target = moved(z, y, x, core)
                    if target is not None:
                        pairs.append((flat_index(z, y, x, core), flat_index(*target)))
    return pairs


def send(array, moved):
    return lax.ppermute(array, every_axis, exchange_pairs(moved))


def to_core(z, y, x, core):
    return z, y, x, 1 - core


def to_near_x(z, y, x, core):
    return z, y, x ^ 3, core


def first_stage(k):
    return lambda z, y, x, core: (z, y, x ^ k, core) if core == 0 else (z, y ^ k, x, core)


def second_stage(k):
    return lambda z, y, x, core: (z, y ^ k, x, core) if core == 0 else (z, y, x ^ k, core)


def along_z(k):
    return lambda z, y, x, core: (z ^ k, y, x, core)


def near_z(z, y, x, core):
    return (z ^ 1 if core == 0 else z ^ 3), y, x, core


def vision_near(k):
    return lambda z, y, x, core: None if core == z % 2 else (z ^ k, y, x, core)


def vision_far(z, y, x, core):
    return (z ^ 2, y, x, 1 - core) if core == z % 2 else None


def to_near_y(z, y, x, core):
    return z, y ^ 1, x, core


params = pltpu.CompilerParams(vmem_limit_bytes=14 * megabyte)
small_params = pltpu.CompilerParams(vmem_limit_bytes=4 * megabyte)
large_params = pltpu.CompilerParams(vmem_limit_bytes=26 * megabyte)
def dot(left, right, left_dim=1, right_dim=0):
    return lax.dot_general(
        left, right, (((left_dim,), (right_dim,)), ((), ())), preferred_element_type=f32
    )


at_near, at_far, at_quarter, at_tensor, at_swapped, at_z, at_core = 0, 1, 2, 3, 7, 8, 9
at_own, at_on_parity, at_row_parity, at_other_order, at_own_order = 10, 11, 12, 13, 29

in_vmem = pl.BlockSpec(memory_space=pltpu.VMEM)
in_smem = pl.BlockSpec(memory_space=pltpu.SMEM)


in_hbm = pl.BlockSpec(memory_space=pltpu.HBM)
anywhere = pl.BlockSpec(memory_space=pl.ANY)


def far_away(array):
    return pltpu.with_memory_space_constraint(array, pltpu.HBM)


def chosen_spec(rows, columns, k, place):
    return pl.BlockSpec(
        (rows, columns), lambda i, table: (0, jnp.where(table[place] == k, i, 0))
    )


token_shape = jax.ShapeDtypeStruct((8, 128), f32)


def cut_features(features, table):
    rows, width = features.shape
    width //= 4
    quarter = rows // 4

    def kernel(table, source, near, far, sems):
        def columns(k):
            return pl.ds(pl.multiple_of(table[k] * width, 128), width)

        lines = pl.ds(pl.multiple_of(table[at_quarter] * quarter, quarter), quarter)
        copies = [
            pltpu.make_async_copy(source.at[lines, columns(at_far)], far, sems.at[0]),
            pltpu.make_async_copy(source.at[:, columns(at_near)], near, sems.at[1]),
        ]
        for copy in copies:
            copy.start()
        for copy in copies:
            copy.wait()

    return pl.pallas_call(
        kernel,
        in_specs=[in_smem, in_hbm],
        out_specs=[in_vmem] * 2,
        out_shape=[jax.ShapeDtypeStruct((r, width), bf16) for r in (rows, quarter)],
        scratch_shapes=[pltpu.SemaphoreType.DMA((2,))],
        compiler_params=small_params,
        name="cut_features",
    )(table, far_away(features))


def mask_rows(ctx_grad, mask):
    def kernel(grad_ref, mask_ref, out):
        out[...] = grad_ref[...] * mask_ref[...].astype(bf16)

    rows, width = ctx_grad.shape
    block = pl.BlockSpec((rows, width // 4), lambda i: (0, i))
    return pl.pallas_call(
        kernel,
        grid=(4,),
        in_specs=[block, pl.BlockSpec((rows, 1), lambda i: (0, 0))],
        out_specs=block,
        out_shape=jax.ShapeDtypeStruct(ctx_grad.shape, bf16),
        compiler_params=small_params,
        name="mask_rows",
    )(ctx_grad, mask)


def project(slices, table, key_proj, value_proj):
    rows, width = slices[0].shape
    columns = key_proj.shape[1]
    n = len(slices)

    def kernel(table, *refs):
        slice_refs, projections, (out, done, held, sems) = refs[:n], refs[n : n + 2], refs[n + 2 :]
        done[...] = jnp.zeros_like(done)
        copies = []
        for i in range(n):
            lines = pl.ds(pl.multiple_of(table[at_tensor + i] * width, width), width)
            for j in range(2):
                copy = pltpu.make_async_copy(projections[j].at[lines, :], held.at[i, j], sems.at[i, j])
                copy.start()
                copies.append(copy)
        for j in range(2):
            total = 0.0
            for i in range(n):
                copies[2 * i + j].wait()
                total += dot(slice_refs[i][...], held[i, j])
            out[:, j * columns : (j + 1) * columns] = total

    return pl.pallas_call(
        kernel,
        in_specs=[in_smem] + [in_vmem] * n + [in_hbm] * 2,
        out_specs=[in_vmem] * 2,
        out_shape=[jax.ShapeDtypeStruct((rows, 2 * columns), f32), token_shape],
        scratch_shapes=[pltpu.VMEM((n, 2, width, columns), bf16), pltpu.SemaphoreType.DMA((n, 2))],
        compiler_params=params,
        name="project",
    )(table, *slices, far_away(key_proj), far_away(value_proj))


def choose(own, other, table):
    def kernel(table, first, second, one, two):
        for k, (a, b) in enumerate(((first, second), (second, first))):

            @pl.when(table[at_swapped] == k)
            def _():
                one[...] = a[...]
                two[...] = b[...]

    return pl.pallas_call(
        kernel,
        in_specs=[in_smem] + [in_vmem] * 2,
        out_specs=[in_vmem] * 2,
        out_shape=[jax.ShapeDtypeStruct(own.shape, bf16)] * 2,
        compiler_params=small_params,
        name="choose",
    )(table, own, other)


def middle(last_slices, raw, queries, masked, gain, key_proj, value_proj, table):
    vis_rows, width = last_slices[0].shape
    depth, columns = key_proj.shape
    kv_heads = columns // head_size
    text_rows = queries.shape[0]
    group = queries.shape[1] // head_size // kv_heads
    group_width = group * head_size
    half = vis_rows // 2
    blocks = 16
    lines = depth // blocks
    unroll = 8

    def kernel(
        table, slice_one, slice_two, raw_ref, gain_ref, query_ref, masked_ref, key_ref, value_ref,
        grads, other_terms, own_terms,
        keys, values, sums, turned,
    ):
        projected = [raw_ref[:, :columns], raw_ref[:, columns:]]
        for i, slice_ref in enumerate((slice_one, slice_two)):
            place = pl.ds(pl.multiple_of(table[at_tensor + 2 + i] * width, width), width)
            projected[0] += dot(slice_ref[...], key_ref[place, :])
            projected[1] += dot(slice_ref[...], value_ref[place, :])
        key_all, value_all = projected[0], projected[1].astype(bf16)
        for head in range(kv_heads):
            lanes = slice(head * head_size, (head + 1) * head_size)
            key_raw = key_all[:, lanes]
            inv_rms = lax.rsqrt(jnp.mean(key_raw * key_raw, -1, keepdims=True) + norm_eps)
            keys[...] = (key_raw * inv_rms * gain_ref[...]).astype(bf16)
            values[...] = value_all[:, lanes]
            sums[...] = jnp.zeros_like(sums)
            def step(i, carry):
                for j in range(unroll):
                    text = (head * group + i * unroll + j) * head_size
                    text = pl.ds(pl.multiple_of(text, head_size), head_size)
                    query = query_ref[:, text]
                    grad = masked_ref[:, text]
                    exp_scores = jnp.exp2(dot(keys[...], query, 1, 1) * (score_scale * log2_e))
                    prob_grad = dot(values[...], grad, 1, 1)
                    probs = exp_scores * (1.0 / jnp.sum(exp_scores, 0, keepdims=True))
                    row_delta = jnp.sum(probs * prob_grad, 0, keepdims=True)
                    sums[1] += dot(probs.astype(bf16), grad)
                    sums[0] += dot((probs * (prob_grad - row_delta)).astype(bf16), query)
                return carry

            lax.fori_loop(0, group // unroll, step, 0)
            scaled = sums[0] * score_scale * gain_ref[...]
            mean = jnp.mean(scaled * key_raw, -1, keepdims=True)
            key_grad = inv_rms * (scaled - key_raw * inv_rms * inv_rms * mean)
            grads[:, lanes] = key_grad.astype(bf16)
            grads[:, columns + head * head_size : columns + (head + 1) * head_size] = sums[1].astype(bf16)

        for i in range(2):
            here = (table[at_core] + i) % 2 * half
            turned[i * half : (i + 1) * half, :] = grads[pl.ds(pl.multiple_of(here, half), half), :]

        def token_step(i, carry):
            here = pl.ds(pl.multiple_of(i * lines, lines), lines)
            other_place = pl.multiple_of(table[at_other_order + i] * lines, lines)
            own_place = pl.multiple_of(table[at_own_order + i] * lines, lines)
            term = dot(key_ref[here, :], turned[:, :columns], 1, 1)
            term += dot(value_ref[here, :], turned[:, columns:], 1, 1)
            own_terms[pl.ds(own_place, lines), :] = term[:, :half].astype(bf16)
            other_terms[pl.ds(other_place, lines), :] = term[:, half:].astype(bf16)
            return carry

        lax.fori_loop(0, blocks, token_step, 0, unroll=4)

    return pl.pallas_call(
        kernel,
        in_specs=[in_smem] + [in_vmem] * 8,
        out_specs=[in_vmem] * 3,
        out_shape=[jax.ShapeDtypeStruct((vis_rows, 2 * columns), bf16)]
        + [jax.ShapeDtypeStruct((depth, half), bf16)] * 2,
        scratch_shapes=[
            pltpu.VMEM((vis_rows, head_size), bf16),
            pltpu.VMEM((vis_rows, head_size), bf16),
            pltpu.VMEM((2, vis_rows, head_size), f32),
            pltpu.VMEM((vis_rows, 2 * columns), bf16),
        ],
        compiler_params=large_params,
        name="middle",
    )(table, *last_slices, raw, gain, queries, masked, key_proj, value_proj)


def wait_for(array, after):
    return pl.pallas_call(
        lambda *refs: None,
        in_specs=[anywhere] * (1 + len(after)),
        out_specs=anywhere,
        out_shape=jax.ShapeDtypeStruct(array.shape, array.dtype),
        input_output_aliases={0: 0},
        compiler_params=small_params,
        name="wait_for",
    )(array, *after)


def add_terms(own_terms, core_terms, after):
    rows, tokens = own_terms.shape
    part = rows // 4

    def kernel(own, other, *rest):
        for i, out in enumerate(rest[-4:]):
            lines = slice(i * part, (i + 1) * part)
            out[...] = (own[lines, :].astype(f32) + other[lines, :].astype(f32)).astype(bf16)

    return pl.pallas_call(
        kernel,
        in_specs=[in_vmem] * 2 + [anywhere] * len(after),
        out_specs=[in_vmem] * 4,
        out_shape=[jax.ShapeDtypeStruct((part, tokens), bf16)] * 4,
        compiler_params=params,
        name="add_terms",
    )(own_terms, core_terms, *after)


def add_first(parts, after):
    rows, tokens = parts[0].shape
    block = rows // 4

    def kernel(*refs):
        own, *outs = refs[-4:]
        for i, out in enumerate((own, *outs)):
            lines = slice(i * block, (i + 1) * block)
            out[...] = sum(ref[lines, :].astype(f32) for ref in refs[:4]).astype(out.dtype)

    return pl.pallas_call(
        kernel,
        in_specs=[in_vmem] * 4 + [anywhere] * len(after),
        out_specs=[in_vmem] * 4,
        out_shape=[jax.ShapeDtypeStruct((block, tokens), f32)]
        + [jax.ShapeDtypeStruct((block, tokens), bf16)] * 3,
        compiler_params=small_params,
        name="add_first",
    )(*parts, *after)


def add_second(own, arrived, table, after):
    rows, tokens = own.shape
    half = rows // 2

    def kernel(table, *refs):
        for i in range(2):
            lines = pl.ds(pl.multiple_of((table[at_core] + i) % 2 * half, half), half)
            total = sum(ref[lines, :].astype(f32) for ref in refs[:4]).astype(bf16)
            refs[-1][i * half : (i + 1) * half, :] = total

    return pl.pallas_call(
        kernel,
        in_specs=[in_smem] + [in_vmem] * 4 + [anywhere] * len(after),
        out_specs=in_vmem,
        out_shape=jax.ShapeDtypeStruct((rows, tokens), bf16),
        compiler_params=small_params,
        name="add_second",
    )(table, own, *arrived, *after)


def weight_grads(gathered, by_z, pairs, table, grads, after):
    rows, width = gathered[0].shape
    columns = grads[0].shape[1] // 2
    steps = 2
    block = width // steps
    choices = [[(at_own, k, v) for k, v in enumerate(gathered)]]
    choices += [
        [(at_on_parity, int(i < 2), by_z[i]), (at_on_parity, int(i == 2), pairs[i])] for i in range(3)
    ]
    flat = sum(choices, [])

    def kernel(table, *refs):
        vision_refs, grad_refs, (key_out, value_out, done, picked) = refs[: len(flat)], refs[len(flat) : -5], refs[-4:]
        done[...] = jnp.zeros_like(done)
        total = 0.0
        at = 0
        for i, options in enumerate(choices):
            for place, value, _ in options:

                @pl.when(table[place] == value)
                def _(ref=vision_refs[at]):
                    picked[i] = ref[...]

                at += 1
        for i in range(4):
            total += dot(picked[i], grad_refs[i][...], 0, 0)
        key_out[...] = total[:, :columns]
        value_out[...] = total[:, columns:]

    return pl.pallas_call(
        kernel,
        grid_spec=pltpu.PrefetchScalarGridSpec(
            num_scalar_prefetch=1,
            grid=(steps,),
            in_specs=[chosen_spec(rows, block, value, place) for place, value, _ in flat]
            + [pl.BlockSpec(g.shape, lambda i, table: (0, 0)) for g in grads]
            + [anywhere],
            out_specs=[pl.BlockSpec((block, columns), lambda i, table: (i, 0))] * 2
            + [pl.BlockSpec(token_shape.shape, lambda i, table: (0, 0))],
            scratch_shapes=[pltpu.VMEM((4, rows, block), bf16)],
        ),
        out_shape=[jax.ShapeDtypeStruct((width, columns), f32)] * 2 + [token_shape],
        compiler_params=large_params,
        name="weight_grads",
    )(table, *[v for _, _, v in flat], *grads, after)


def turn_features(features, near, near_pair, far, table, after):
    rows, width = near.shape
    quarter = rows // 4
    steps = 1
    block = width // steps

    def kernel(table, own_ref, near_ref, near_pair_ref, *rest):
        out, done, joined = rest[-3:]
        done[...] = jnp.zeros_like(done)
        for i, ref in enumerate(rest[:4]):
            place = (table[at_core] + i // 2) % 2 * 2 + (table[at_row_parity] + i % 2) % 2
            joined[pl.ds(pl.multiple_of(place * quarter, quarter), quarter), :] = ref[...]
        for i, ref in enumerate((own_ref, near_ref, near_pair_ref, joined)):
            out[:, i * rows : (i + 1) * rows] = ref[...].T

    return pl.pallas_call(
        kernel,
        grid_spec=pltpu.PrefetchScalarGridSpec(
            num_scalar_prefetch=1,
            grid=(steps,),
            in_specs=[pl.BlockSpec((rows, block), lambda i, table: (0, table[at_z] * steps + i))]
            + [pl.BlockSpec((rows, block), lambda i, table: (0, i))] * 2
            + [pl.BlockSpec((quarter, block), lambda i, table: (0, i))] * 4
            + [anywhere],
            out_specs=[
                pl.BlockSpec((block, 4 * rows), lambda i, table: (i, 0)),
                pl.BlockSpec(token_shape.shape, lambda i, table: (0, 0)),
            ],
            scratch_shapes=[pltpu.VMEM((rows, block), bf16)],
        ),
        out_shape=[jax.ShapeDtypeStruct((width, 4 * rows), bf16), token_shape],
        compiler_params=large_params,
        name="turn_features",
    )(table, far_away(features), near, near_pair, *far, after)


def projector_grad(turned, tokens, partners, table, after):
    width, depth = turned.shape
    rows, half = tokens[0].shape
    columns = rows // 2
    steps = 5
    block = width // steps

    def kernel(table, feature_ref, *refs):
        out, joined, total, sems = refs[-4:]
        for k in range(2):

            @pl.when(table[at_core] == k)
            def _():
                for i, image in enumerate((0, 1, 3, 2) if k == 0 else (0, 3, 1, 2)):
                    joined[:, (2 * i + k) * half : (2 * i + k + 1) * half] = refs[image][:columns, :]
                    joined[:, (2 * i + 1 - k) * half : (2 * i + 2 - k) * half] = refs[4 + image][
                        columns:, :
                    ]

        copies = []
        for step in range(steps):
            lines = pl.ds(step * block, block)
            total[lines, :] = dot(feature_ref[lines, :], joined[...], 1, 1)
            copies.append(pltpu.make_async_copy(total.at[lines, :], out.at[lines, :], sems.at[step]))
            copies[-1].start()
        for copy in copies:
            copy.wait()

    return pl.pallas_call(
        kernel,
        in_specs=[in_smem] + [in_vmem] * 9 + [anywhere],
        out_specs=in_hbm,
        out_shape=pltpu.HBM((width, columns), f32),
        scratch_shapes=[
            pltpu.VMEM((columns, depth), bf16),
            pltpu.VMEM((width, columns), f32),
            pltpu.SemaphoreType.DMA((steps,)),
        ],
        compiler_params=params,
        name="projector_grad",
    )(table, turned, *tokens, *partners, after)


def integers(z, pipe, tensor):
    y, core = pipe // 2, tensor % 2
    x = (tensor // 2) * 2 + pipe % 2
    on_parity = (core == z % 2).astype(jnp.int32)
    values = [jnp.where(core == 0, z ^ 1, z ^ 3), z ^ 2, 2 * core + y % 2]
    values += [tensor, tensor ^ 1, tensor ^ 2, tensor ^ 3]
    values += [(tensor // 2 == z // 2).astype(jnp.int32) ^ (1 - on_parity), z, core]
    values += [z ^ tensor, on_parity, y % 2]
    for this_core in (1 - core, core):
        for block in range(16):
            across_y, across_x = y ^ (block // 4), x ^ (block % 2 * 2 + block // 2 % 2)
            values.append(
                jnp.where(this_core == 0, across_x * 4 + across_y, across_y * 4 + across_x)
            )
    return jnp.stack(values).astype(jnp.int32)


def shards(vision, features, queries, ctx_grad, row_mask, key_weight, value_weight, key_gain):
    key_proj, value_proj = key_weight[0], value_weight[0]
    table = integers(lax.axis_index("dp"), lax.axis_index("pipe"), lax.axis_index("tensor"))

    from_core = send(vision, to_core)
    from_x = send(vision, to_near_x)

    feature_near, feature_far = cut_features(features, table)
    feature_near = send(feature_near, near_z)
    feature_far = send(feature_far, along_z(2))

    masked = mask_rows(ctx_grad, row_mask[:, None])
    raw, done = project([vision, from_core], table, key_proj, value_proj)
    from_x = wait_for(from_x, [done, masked, feature_near, feature_far])
    from_xc = send(from_x, to_core)
    vision_one, vision_two = choose(vision, from_x, table)
    gathered = [vision, from_core, from_x, from_xc]
    by_z = [send(vision_one, vision_near(1)), send(vision_two, vision_near(3))]
    feature_far = [feature_far, send(feature_far, to_near_y)]
    grads, other_terms, own_terms = middle(
        [from_x, from_xc], raw, queries, masked, key_gain, key_proj, value_proj, table
    )

    core_terms = send(wait_for(other_terms, by_z + feature_far), to_core)
    by_z.append(send(vision_one, vision_far))
    feature_far += [send(part, to_core) for part in feature_far]
    terms = add_terms(own_terms, core_terms, feature_far)
    arrived = [send(terms[i], first_stage(i)) for i in (2, 1, 3)]
    grads_z = {i: send(grads, along_z(i)) for i in (1, 2, 3)}
    own, *partial = add_first([terms[0], *arrived], [by_z[2], grads_z[2]])
    arrived = [send(partial[i - 1], second_stage(i)) for i in (2, 1, 3)]
    feature_near = wait_for(feature_near, [own])
    feature_pair = send(feature_near, to_core)
    turned, done = turn_features(features, feature_near, feature_pair, feature_far, table, own)
    token = add_second(own, arrived, table, [done, grads_z[1], grads_z[3]])
    tokens = [token, *(send(token, along_z(i)) for i in (1, 2, 3))]
    by_z = [wait_for(array, [token]) for array in by_z]
    pairs = [send(array, to_core) for array in by_z]
    key_total, value_total, done = weight_grads(
        gathered, by_z, pairs, table, [grads, *(grads_z[i] for i in (1, 3, 2))], token
    )
    tokens[1:] = [wait_for(array, [done]) for array in tokens[1:]]
    partners = [send(array, to_core) for array in tokens]
    projector_total = projector_grad(turned, tokens, partners, table, done)
    return (key_total[None], value_total[None], projector_total)


def solution(mesh):
    in_specs = (
        P("dp", "tensor"),
        P("dp", None),
        P("dp", "tensor"),
        P("dp", "tensor"),
        P("dp"),
        P("pipe", None, "tensor"),
        P("pipe", None, "tensor"),
        P("pipe", None),
    )
    out_specs = (P("pipe", "dp", "tensor"), P("pipe", "dp", "tensor"), P("dp", ("pipe", "tensor")))
    return jax.shard_map(shards, mesh=mesh, in_specs=in_specs, out_specs=out_specs, check_vma=False)
```

```python
import jax
import jax.numpy as jnp
from jax import lax
from jax.experimental import pallas as pl
from jax.experimental.pallas import tpu as pltpu
from jax.sharding import PartitionSpec as P

norm_eps = 1e-05
every_axis = ("dp", "pipe", "tensor")
bf16 = jnp.bfloat16
f32 = jnp.float32
head_size = 128
score_scale = head_size**-0.5
log2_e = 1.4426950408889634
megabyte = 2**20


def flat_index(z, y, x, core):
    return z * 32 + y * 8 + (x & 1) * 4 + (x >> 1) * 2 + core


def exchange_pairs(moved):
    pairs = []
    for z in range(4):
        for y in range(4):
            for x in range(4):
                for core in range(2):
                    target = moved(z, y, x, core)
                    if target is not None:
                        pairs.append((flat_index(z, y, x, core), flat_index(*target)))
    return pairs


def send(array, moved):
    return lax.ppermute(array, every_axis, exchange_pairs(moved))


def to_core(z, y, x, core):
    return z, y, x, 1 - core


def to_near_x(z, y, x, core):
    return z, y, x ^ 3, core


def first_stage(k):
    return lambda z, y, x, core: (z, y, x ^ k, core) if core == 0 else (z, y ^ k, x, core)


def second_stage(k):
    return lambda z, y, x, core: (z, y ^ k, x, core) if core == 0 else (z, y, x ^ k, core)


def along_z(k):
    return lambda z, y, x, core: (z ^ k, y, x, core)


def near_z(z, y, x, core):
    return (z ^ 1 if core == 0 else z ^ 3), y, x, core


def vision_near(k):
    return lambda z, y, x, core: None if core == z % 2 else (z ^ k, y, x, core)


def vision_far(z, y, x, core):
    return (z ^ 2, y, x, 1 - core) if core == z % 2 else None


def to_near_y(z, y, x, core):
    return z, y ^ 1, x, core


params = pltpu.CompilerParams(vmem_limit_bytes=14 * megabyte)
small_params = pltpu.CompilerParams(vmem_limit_bytes=4 * megabyte)
large_params = pltpu.CompilerParams(vmem_limit_bytes=26 * megabyte)
def dot(left, right, left_dim=1, right_dim=0):
    return lax.dot_general(
        left, right, (((left_dim,), (right_dim,)), ((), ())), preferred_element_type=f32
    )


at_near, at_far, at_quarter, at_tensor, at_swapped, at_z, at_core = 0, 1, 2, 3, 7, 8, 9
at_own, at_on_parity, at_row_parity, at_other_order, at_own_order = 10, 11, 12, 13, 29

in_vmem = pl.BlockSpec(memory_space=pltpu.VMEM)
in_smem = pl.BlockSpec(memory_space=pltpu.SMEM)


in_hbm = pl.BlockSpec(memory_space=pltpu.HBM)
anywhere = pl.BlockSpec(memory_space=pl.ANY)


def far_away(array):
    return pltpu.with_memory_space_constraint(array, pltpu.HBM)


def chosen_spec(rows, columns, k, place):
    return pl.BlockSpec(
        (rows, columns), lambda i, table: (0, jnp.where(table[place] == k, i, 0))
    )


token_shape = jax.ShapeDtypeStruct((8, 128), f32)


def cut_features(features, table):
    rows, width = features.shape
    width //= 4
    quarter = rows // 4

    def kernel(table, source, near, far, sems):
        def columns(k):
            return pl.ds(pl.multiple_of(table[k] * width, 128), width)

        lines = pl.ds(pl.multiple_of(table[at_quarter] * quarter, quarter), quarter)
        copies = [pltpu.make_async_copy(source.at[lines, columns(at_far)], far, sems.at[4])]
        for i in range(4):
            part = pl.ds(i * quarter, quarter)
            copies.append(
                pltpu.make_async_copy(
                    source.at[part, columns(at_near)], near.at[part, :], sems.at[i]
                )
            )
        for copy in copies:
            copy.start()
        for copy in copies:
            copy.wait()

    return pl.pallas_call(
        kernel,
        in_specs=[in_smem, in_hbm],
        out_specs=[in_vmem] * 2,
        out_shape=[jax.ShapeDtypeStruct((r, width), bf16) for r in (rows, quarter)],
        scratch_shapes=[pltpu.SemaphoreType.DMA((5,))],
        compiler_params=small_params,
        name="cut_features",
    )(table, far_away(features))


def mask_rows(ctx_grad, mask):
    def kernel(grad_ref, mask_ref, out):
        out[...] = grad_ref[...] * mask_ref[...].astype(bf16)

    rows, width = ctx_grad.shape
    block = pl.BlockSpec((rows, width // 4), lambda i: (0, i))
    return pl.pallas_call(
        kernel,
        grid=(4,),
        in_specs=[block, pl.BlockSpec((rows, 1), lambda i: (0, 0))],
        out_specs=block,
        out_shape=jax.ShapeDtypeStruct(ctx_grad.shape, bf16),
        compiler_params=small_params,
        name="mask_rows",
    )(ctx_grad, mask)


def project(slices, table, key_proj, value_proj):
    rows, width = slices[0].shape
    columns = key_proj.shape[1]
    n = len(slices)

    def kernel(table, *refs):
        slice_refs, projections, (out, done, held, sems) = refs[:n], refs[n : n + 2], refs[n + 2 :]
        done[...] = jnp.zeros_like(done)
        copies = []
        for i in range(n):
            lines = pl.ds(pl.multiple_of(table[at_tensor + i] * width, width), width)
            for j in range(2):
                copy = pltpu.make_async_copy(projections[j].at[lines, :], held.at[i, j], sems.at[i, j])
                copy.start()
                copies.append(copy)
        for j in range(2):
            total = 0.0
            for i in range(n):
                copies[2 * i + j].wait()
                total += dot(slice_refs[i][...], held[i, j])
            out[:, j * columns : (j + 1) * columns] = total

    return pl.pallas_call(
        kernel,
        in_specs=[in_smem] + [in_vmem] * n + [in_hbm] * 2,
        out_specs=[in_vmem] * 2,
        out_shape=[jax.ShapeDtypeStruct((rows, 2 * columns), f32), token_shape],
        scratch_shapes=[pltpu.VMEM((n, 2, width, columns), bf16), pltpu.SemaphoreType.DMA((n, 2))],
        compiler_params=params,
        name="project",
    )(table, *slices, far_away(key_proj), far_away(value_proj))


def choose(own, other, table):
    def kernel(table, first, second, one, two):
        for k, (a, b) in enumerate(((first, second), (second, first))):

            @pl.when(table[at_swapped] == k)
            def _():
                one[...] = a[...]
                two[...] = b[...]

    return pl.pallas_call(
        kernel,
        in_specs=[in_smem] + [in_vmem] * 2,
        out_specs=[in_vmem] * 2,
        out_shape=[jax.ShapeDtypeStruct(own.shape, bf16)] * 2,
        compiler_params=small_params,
        name="choose",
    )(table, own, other)


def middle(last_slices, raw, queries, masked, gain, key_proj, value_proj, table):
    vis_rows, width = last_slices[0].shape
    depth, columns = key_proj.shape
    kv_heads = columns // head_size
    text_rows = queries.shape[0]
    group = queries.shape[1] // head_size // kv_heads
    group_width = group * head_size
    half = vis_rows // 2
    blocks = 16
    lines = depth // blocks
    unroll = 8

    def kernel(
        table, slice_one, slice_two, raw_ref, gain_ref, query_ref, masked_ref, key_ref, value_ref,
        grads, other_terms, own_terms,
        keys, values, sums, turned,
    ):
        projected = [raw_ref[:, :columns], raw_ref[:, columns:]]
        for i, slice_ref in enumerate((slice_one, slice_two)):
            place = pl.ds(pl.multiple_of(table[at_tensor + 2 + i] * width, width), width)
            projected[0] += dot(slice_ref[...], key_ref[place, :])
            projected[1] += dot(slice_ref[...], value_ref[place, :])
        key_all, value_all = projected[0], projected[1].astype(bf16)
        for head in range(kv_heads):
            lanes = slice(head * head_size, (head + 1) * head_size)
            key_raw = key_all[:, lanes]
            inv_rms = lax.rsqrt(jnp.mean(key_raw * key_raw, -1, keepdims=True) + norm_eps)
            keys[...] = (key_raw * inv_rms * gain_ref[...]).astype(bf16)
            values[...] = value_all[:, lanes]
            sums[...] = jnp.zeros_like(sums)
            def step(i, carry):
                for j in range(unroll):
                    text = (head * group + i * unroll + j) * head_size
                    text = pl.ds(pl.multiple_of(text, head_size), head_size)
                    query = query_ref[:, text]
                    grad = masked_ref[:, text]
                    exp_scores = jnp.exp2(dot(keys[...], query, 1, 1) * (score_scale * log2_e))
                    prob_grad = dot(values[...], grad, 1, 1)
                    probs = exp_scores * (1.0 / jnp.sum(exp_scores, 0, keepdims=True))
                    row_delta = jnp.sum(probs * prob_grad, 0, keepdims=True)
                    sums[1] += dot(probs.astype(bf16), grad)
                    sums[0] += dot((probs * (prob_grad - row_delta)).astype(bf16), query)
                return carry

            lax.fori_loop(0, group // unroll, step, 0)
            scaled = sums[0] * score_scale * gain_ref[...]
            mean = jnp.mean(scaled * key_raw, -1, keepdims=True)
            key_grad = inv_rms * (scaled - key_raw * inv_rms * inv_rms * mean)
            grads[:, lanes] = key_grad.astype(bf16)
            grads[:, columns + head * head_size : columns + (head + 1) * head_size] = sums[1].astype(bf16)

        for i in range(2):
            here = (table[at_core] + i) % 2 * half
            turned[i * half : (i + 1) * half, :] = grads[pl.ds(pl.multiple_of(here, half), half), :]

        def token_step(i, carry):
            here = pl.ds(pl.multiple_of(i * lines, lines), lines)
            other_place = pl.multiple_of(table[at_other_order + i] * lines, lines)
            own_place = pl.multiple_of(table[at_own_order + i] * lines, lines)
            term = dot(key_ref[here, :], turned[:, :columns], 1, 1)
            term += dot(value_ref[here, :], turned[:, columns:], 1, 1)
            own_terms[pl.ds(own_place, lines), :] = term[:, :half].astype(bf16)
            other_terms[pl.ds(other_place, lines), :] = term[:, half:].astype(bf16)
            return carry

        lax.fori_loop(0, blocks, token_step, 0, unroll=4)

    return pl.pallas_call(
        kernel,
        in_specs=[in_smem] + [in_vmem] * 8,
        out_specs=[in_vmem] * 3,
        out_shape=[jax.ShapeDtypeStruct((vis_rows, 2 * columns), bf16)]
        + [jax.ShapeDtypeStruct((depth, half), bf16)] * 2,
        scratch_shapes=[
            pltpu.VMEM((vis_rows, head_size), bf16),
            pltpu.VMEM((vis_rows, head_size), bf16),
            pltpu.VMEM((2, vis_rows, head_size), f32),
            pltpu.VMEM((vis_rows, 2 * columns), bf16),
        ],
        compiler_params=large_params,
        name="middle",
    )(table, *last_slices, raw, gain, queries, masked, key_proj, value_proj)


def wait_for(array, after):
    return pl.pallas_call(
        lambda *refs: None,
        in_specs=[anywhere] * (1 + len(after)),
        out_specs=anywhere,
        out_shape=jax.ShapeDtypeStruct(array.shape, array.dtype),
        input_output_aliases={0: 0},
        compiler_params=small_params,
        name="wait_for",
    )(array, *after)


def add_terms(own_terms, core_terms, after):
    rows, tokens = own_terms.shape
    part = rows // 4

    def kernel(own, other, *rest):
        for i, out in enumerate(rest[-4:]):
            lines = slice(i * part, (i + 1) * part)
            out[...] = (own[lines, :].astype(f32) + other[lines, :].astype(f32)).astype(bf16)

    return pl.pallas_call(
        kernel,
        in_specs=[in_vmem] * 2 + [anywhere] * len(after),
        out_specs=[in_vmem] * 4,
        out_shape=[jax.ShapeDtypeStruct((part, tokens), bf16)] * 4,
        compiler_params=params,
        name="add_terms",
    )(own_terms, core_terms, *after)


def add_first(parts, after):
    rows, tokens = parts[0].shape
    block = rows // 4

    def kernel(*refs):
        own, *outs = refs[-4:]
        for i, out in enumerate((own, *outs)):
            lines = slice(i * block, (i + 1) * block)
            out[...] = sum(ref[lines, :].astype(f32) for ref in refs[:4]).astype(out.dtype)

    return pl.pallas_call(
        kernel,
        in_specs=[in_vmem] * 4 + [anywhere] * len(after),
        out_specs=[in_vmem] * 4,
        out_shape=[jax.ShapeDtypeStruct((block, tokens), f32)]
        + [jax.ShapeDtypeStruct((block, tokens), bf16)] * 3,
        compiler_params=small_params,
        name="add_first",
    )(*parts, *after)


def add_second(own, arrived, table, after):
    rows, tokens = own.shape
    half = rows // 2

    def kernel(table, *refs):
        for i in range(2):
            lines = pl.ds(pl.multiple_of((table[at_core] + i) % 2 * half, half), half)
            total = sum(ref[lines, :].astype(f32) for ref in refs[:4]).astype(bf16)
            refs[-1][i * half : (i + 1) * half, :] = total

    return pl.pallas_call(
        kernel,
        in_specs=[in_smem] + [in_vmem] * 4 + [anywhere] * len(after),
        out_specs=in_vmem,
        out_shape=jax.ShapeDtypeStruct((rows, tokens), bf16),
        compiler_params=small_params,
        name="add_second",
    )(table, own, *arrived, *after)


def weight_grads(gathered, by_z, pairs, table, grads, after):
    rows, width = gathered[0].shape
    columns = grads[0].shape[1] // 2
    steps = 2
    block = width // steps
    choices = [[(at_own, k, v) for k, v in enumerate(gathered)]]
    choices += [
        [(at_on_parity, int(i < 2), by_z[i]), (at_on_parity, int(i == 2), pairs[i])] for i in range(3)
    ]
    flat = sum(choices, [])

    def kernel(table, *refs):
        vision_refs, grad_refs, (key_out, value_out, done, picked) = refs[: len(flat)], refs[len(flat) : -5], refs[-4:]
        done[...] = jnp.zeros_like(done)
        total = 0.0
        at = 0
        for i, options in enumerate(choices):
            for place, value, _ in options:

                @pl.when(table[place] == value)
                def _(ref=vision_refs[at]):
                    picked[i] = ref[...]

                at += 1
        for i in range(4):
            total += dot(picked[i], grad_refs[i][...], 0, 0)
        key_out[...] = total[:, :columns]
        value_out[...] = total[:, columns:]

    return pl.pallas_call(
        kernel,
        grid_spec=pltpu.PrefetchScalarGridSpec(
            num_scalar_prefetch=1,
            grid=(steps,),
            in_specs=[chosen_spec(rows, block, value, place) for place, value, _ in flat]
            + [pl.BlockSpec(g.shape, lambda i, table: (0, 0)) for g in grads]
            + [anywhere],
            out_specs=[pl.BlockSpec((block, columns), lambda i, table: (i, 0))] * 2
            + [pl.BlockSpec(token_shape.shape, lambda i, table: (0, 0))],
            scratch_shapes=[pltpu.VMEM((4, rows, block), bf16)],
        ),
        out_shape=[jax.ShapeDtypeStruct((width, columns), f32)] * 2 + [token_shape],
        compiler_params=large_params,
        name="weight_grads",
    )(table, *[v for _, _, v in flat], *grads, after)


def turn_features(features, near, near_pair, far, table, after):
    rows, width = near.shape
    quarter = rows // 4
    steps = 1
    block = width // steps

    def kernel(table, own_ref, near_ref, near_pair_ref, *rest):
        out, done, joined = rest[-3:]
        done[...] = jnp.zeros_like(done)
        for i, ref in enumerate(rest[:4]):
            place = (table[at_core] + i // 2) % 2 * 2 + (table[at_row_parity] + i % 2) % 2
            joined[pl.ds(pl.multiple_of(place * quarter, quarter), quarter), :] = ref[...]
        for i, ref in enumerate((own_ref, near_ref, near_pair_ref, joined)):
            out[:, i * rows : (i + 1) * rows] = ref[...].T

    return pl.pallas_call(
        kernel,
        grid_spec=pltpu.PrefetchScalarGridSpec(
            num_scalar_prefetch=1,
            grid=(steps,),
            in_specs=[pl.BlockSpec((rows, block), lambda i, table: (0, table[at_z] * steps + i))]
            + [pl.BlockSpec((rows, block), lambda i, table: (0, i))] * 2
            + [pl.BlockSpec((quarter, block), lambda i, table: (0, i))] * 4
            + [anywhere],
            out_specs=[
                pl.BlockSpec((block, 4 * rows), lambda i, table: (i, 0)),
                pl.BlockSpec(token_shape.shape, lambda i, table: (0, 0)),
            ],
            scratch_shapes=[pltpu.VMEM((rows, block), bf16)],
        ),
        out_shape=[jax.ShapeDtypeStruct((width, 4 * rows), bf16), token_shape],
        compiler_params=large_params,
        name="turn_features",
    )(table, far_away(features), near, near_pair, *far, after)


def projector_grad(turned, tokens, partners, table, after):
    width, depth = turned.shape
    rows, half = tokens[0].shape
    columns = rows // 2
    steps = 5
    block = width // steps

    def kernel(table, feature_ref, *refs):
        out, joined, total, sems = refs[-4:]
        for k in range(2):

            @pl.when(table[at_core] == k)
            def _():
                for i, image in enumerate((0, 1, 3, 2) if k == 0 else (0, 3, 1, 2)):
                    joined[:, (2 * i + k) * half : (2 * i + k + 1) * half] = refs[image][:columns, :]
                    joined[:, (2 * i + 1 - k) * half : (2 * i + 2 - k) * half] = refs[4 + image][
                        columns:, :
                    ]

        copies = []
        for step in range(steps):
            lines = pl.ds(step * block, block)
            total[lines, :] = dot(feature_ref[lines, :], joined[...], 1, 1)
            copies.append(pltpu.make_async_copy(total.at[lines, :], out.at[lines, :], sems.at[step]))
            copies[-1].start()
        for copy in copies:
            copy.wait()

    return pl.pallas_call(
        kernel,
        in_specs=[in_smem] + [in_vmem] * 9 + [anywhere],
        out_specs=in_hbm,
        out_shape=pltpu.HBM((width, columns), f32),
        scratch_shapes=[
            pltpu.VMEM((columns, depth), bf16),
            pltpu.VMEM((width, columns), f32),
            pltpu.SemaphoreType.DMA((steps,)),
        ],
        compiler_params=params,
        name="projector_grad",
    )(table, turned, *tokens, *partners, after)


def integers(z, pipe, tensor):
    y, core = pipe // 2, tensor % 2
    x = (tensor // 2) * 2 + pipe % 2
    on_parity = (core == z % 2).astype(jnp.int32)
    values = [jnp.where(core == 0, z ^ 1, z ^ 3), z ^ 2, 2 * core + y % 2]
    values += [tensor, tensor ^ 1, tensor ^ 2, tensor ^ 3]
    values += [(tensor // 2 == z // 2).astype(jnp.int32) ^ (1 - on_parity), z, core]
    values += [z ^ tensor, on_parity, y % 2]
    for this_core in (1 - core, core):
        for block in range(16):
            across_y, across_x = y ^ (block // 4), x ^ (block % 2 * 2 + block // 2 % 2)
            values.append(
                jnp.where(this_core == 0, across_x * 4 + across_y, across_y * 4 + across_x)
            )
    return jnp.stack(values).astype(jnp.int32)


def shards(vision, features, queries, ctx_grad, row_mask, key_weight, value_weight, key_gain):
    key_proj, value_proj = key_weight[0], value_weight[0]
    table = integers(lax.axis_index("dp"), lax.axis_index("pipe"), lax.axis_index("tensor"))

    from_core = send(vision, to_core)
    from_x = send(vision, to_near_x)

    feature_near, feature_far = cut_features(features, table)
    feature_near = send(feature_near, near_z)
    feature_far = send(feature_far, along_z(2))

    masked = mask_rows(ctx_grad, row_mask[:, None])
    raw, done = project([vision, from_core], table, key_proj, value_proj)
    from_x = wait_for(from_x, [done, masked, feature_near, feature_far])
    from_xc = send(from_x, to_core)
    vision_one, vision_two = choose(vision, from_x, table)
    gathered = [vision, from_core, from_x, from_xc]
    by_z = [send(vision_one, vision_near(1)), send(vision_two, vision_near(3))]
    feature_far = [feature_far, send(feature_far, to_near_y)]
    grads, other_terms, own_terms = middle(
        [from_x, from_xc], raw, queries, masked, key_gain, key_proj, value_proj, table
    )

    core_terms = send(wait_for(other_terms, by_z + feature_far), to_core)
    by_z.append(send(vision_one, vision_far))
    feature_far += [send(part, to_core) for part in feature_far]
    terms = add_terms(own_terms, core_terms, feature_far)
    arrived = [send(terms[i], first_stage(i)) for i in (2, 1, 3)]
    grads_z = {i: send(grads, along_z(i)) for i in (1, 2, 3)}
    own, *partial = add_first([terms[0], *arrived], [by_z[2], grads_z[2]])
    arrived = [send(partial[i - 1], second_stage(i)) for i in (2, 1, 3)]
    feature_near = wait_for(feature_near, [own])
    feature_pair = send(feature_near, to_core)
    turned, done = turn_features(features, feature_near, feature_pair, feature_far, table, own)
    token = add_second(own, arrived, table, [done, grads_z[1], grads_z[3]])
    tokens = [token, *(send(token, along_z(i)) for i in (1, 2, 3))]
    by_z = [wait_for(array, [token]) for array in by_z]
    pairs = [send(array, to_core) for array in by_z]
    key_total, value_total, done = weight_grads(
        gathered, by_z, pairs, table, [grads, *(grads_z[i] for i in (1, 3, 2))], token
    )
    tokens[1:] = [wait_for(array, [done]) for array in tokens[1:]]
    partners = [send(array, to_core) for array in tokens]
    projector_total = projector_grad(turned, tokens, partners, table, done)
    return (key_total[None], value_total[None], projector_total)


def solution(mesh):
    in_specs = (
        P("dp", "tensor"),
        P("dp", None),
        P("dp", "tensor"),
        P("dp", "tensor"),
        P("dp"),
        P("pipe", None, "tensor"),
        P("pipe", None, "tensor"),
        P("pipe", None),
    )
    out_specs = (P("pipe", "dp", "tensor"), P("pipe", "dp", "tensor"), P("dp", ("pipe", "tensor")))
    return jax.shard_map(shards, mesh=mesh, in_specs=in_specs, out_specs=out_specs, check_vma=False)
```
